512 devices in a mesh: seq: 32 (over z_hi, x, core), head: 16 (over z_lo, y).
Axes of the slice: x: 4, y: 8, z: 8 (z_hi: 4, z_lo: 2; z = z_hi * 2 + z_lo), core: 2. Of those that a mesh axis runs over, the one named last changes fastest.
Arguments:
- queries: bfloat16 [1024, 128, 576], P('seq', 'head'), may hold values from -1024 to 1024
- latents: bfloat16 [4096, 576], P('seq'), may hold values from -6 to 6
- out_grad: bfloat16 [1024, 128, 512], P('seq', 'head'), may hold values from -6 to 6
- layer_out: bfloat16 [1024, 128, 512], P('seq', 'head'), may hold values from -4 to 4
- query_start: int32 [32], P('seq'), may hold values from 0 to 4095, as said below
Outputs:
- query_grad: bfloat16 [1024, 128, 576], P('seq', 'head')
- latent_grad: float32 [4096, 576], P(('seq', 'head'))
The draws below stay inside these ranges and needn't reach their ends.
Inputs may be any that keep to these rules, and one draw needn't show every extreme that they name: Shard i holds the 32 queries at consecutive positions from query_start[i]; queries past the last latent position see every latent row.
All inputs are finite; a program needn't handle non-finite values.
Results may differ from the reference program's by a relative error of at most 0.0049.
Values may be sent and summed in bfloat16 or wider, within the bound.
No kernel may reach another device: no remote copies, remote signals or barrier semaphores. Data moves between devices by JAX's collectives and lax.ppermute only.
A program may use at most 64 MiB of HBM per device.

```python
import jax
import jax.numpy as jnp
from jax import lax

HEADS = 128
DL = 512
DR = 64
Q_DEV = 32
DK = 576
QUERIES = 1024
S_TOTAL = 4096
SHARDS = 32


def shared_draw(key):
    latent_key = jax.random.fold_in(key, 11)
    query_key = jax.random.fold_in(key, 12)
    latent_rows = jax.random.normal(latent_key, (S_TOTAL, DK), jnp.float32)
    query_rows = jax.random.normal(query_key, (QUERIES, HEADS, DK), jnp.float32)
    latent_rows = jnp.clip(latent_rows, -6.0, 6.0)
    query_rows = jnp.clip(query_rows, -1024.0, 1024.0)
    return (latent_rows, query_rows)


def draw_queries(key, part):
    return shared_draw(key)[1].astype(jnp.bfloat16)


def draw_latents(key, part):
    return shared_draw(key)[0].astype(jnp.bfloat16)


def draw_query_start(key, part):
    starts = jax.random.randint(jax.random.fold_in(key, 21), (SHARDS,), 0, S_TOTAL, jnp.int32)
    order = jax.random.permutation(jax.random.fold_in(key, 22), SHARDS)
    starts = starts.at[order[0]].set(0)
    starts = starts.at[order[1]].set(S_TOTAL - 1)
    return starts.astype(jnp.int32)


def shard_levels(rng, shape, pieces, smallest, top_value):
    loudness, own = 1.0, jax.random.fold_in(rng, 6)
    for position, blocks in pieces:
        draws = jnp.exp(jax.random.uniform(jax.random.fold_in(own, position), (blocks,), jnp.float32, smallest / len(pieces), top_value / len(pieces)))
        loudness = loudness * jnp.repeat(draws, shape[position] // blocks).reshape([-1 if axis == position else 1 for axis in range(len(shape))])
    return loudness


def normal_values(rng, extent, spread, reach, shards=(), held_as=jnp.bfloat16):
    result = spread * jax.random.normal(rng, extent, jnp.float32)
    if shards:
        result = result * shard_levels(rng, extent, shards, -0.22, 0.18)
    return jnp.clip(result, -reach, reach).astype(held_as)


def setup_inputs(seed: int = 0) -> dict:
    key_of = jax.random.split(jax.random.key(seed), 6)
    return {
        "queries": draw_queries(jax.random.fold_in(key_of[5], 71), 0),
        "latents": draw_latents(jax.random.fold_in(key_of[5], 71), 0),
        "out_grad": normal_values(key_of[2], (QUERIES, HEADS, DL), 1.0, 6.0, ((0, 32), (1, 16))),
        "layer_out": normal_values(key_of[3], (QUERIES, HEADS, DL), 0.5, 4.0, ((0, 32), (1, 16))),
        "query_start": draw_query_start(jax.random.fold_in(key_of[5], 71), 0),
    }


score_scale = 192 ** -0.5


def reference(queries, latents, out_grad, layer_out, query_start):
    query_pos = (query_start[:, None] + jnp.arange(Q_DEV, dtype=jnp.int32)[None, :]).reshape(-1)
    key_pos = jnp.arange(S_TOTAL, dtype=jnp.int32)
    visible = key_pos[None, :] <= query_pos[:, None]
    row_delta = jnp.sum(out_grad.astype(jnp.float32) * layer_out.astype(jnp.float32), axis=2)
    values = latents[:, :DL]

    def per_head(grad_sum, head_items):
        head_query, head_grad, head_delta = head_items
        scores = jnp.dot(head_query, latents.T, preferred_element_type=jnp.float32) * score_scale
        scores = jnp.where(visible, scores, -jnp.inf)
        top = jnp.max(scores, axis=1, keepdims=True)
        log_norm = top + jnp.log(jnp.sum(jnp.exp(scores - top), axis=1, keepdims=True))
        weights = jnp.exp(scores - log_norm)
        prob_grad = jnp.dot(head_grad, values.T, preferred_element_type=jnp.float32)
        dscore = (score_scale * weights * (prob_grad - head_delta[:, None])).astype(jnp.bfloat16)
        query_term = jnp.dot(dscore, latents, preferred_element_type=jnp.float32)
        key_term = jnp.dot(dscore.T, head_query, preferred_element_type=jnp.float32)
        value_term = jnp.dot(weights.astype(jnp.bfloat16).T, head_grad, preferred_element_type=jnp.float32)
        key_term = key_term + jnp.pad(value_term, ((0, 0), (0, DR)))
        return grad_sum + key_term, query_term.astype(jnp.bfloat16)

    start_sum = jnp.zeros((S_TOTAL, DK), jnp.float32)
    latent_grad, query_terms = lax.scan(
        per_head, start_sum,
        (jnp.moveaxis(queries, 1, 0), jnp.moveaxis(out_grad, 1, 0), row_delta.T))
    query_grad = jnp.moveaxis(query_terms, 0, 1)
    return query_grad, latent_grad
```

```python
import jax
import jax.numpy as jnp
from jax import lax
from jax.experimental import pallas as pl
from jax.experimental.pallas import tpu as pltpu
from jax.sharding import Mesh, PartitionSpec as P

score_scale = 192 ** (-0.5)
masked_score = -1e30
least_top = -1e29

ROWS = 256
WIDE = 640
VALUES = 512
PACK = 1152
KEYS = 1024
TILE = 128
TEAM = 4

FINE = ("zh", "x", "c", "zl", "yh", "y0")


def prep_kernel(start_ref, q_ref, do_ref, lo_ref, out_ref):
    grad = do_ref[...]
    delta = jnp.sum(
        grad.astype(jnp.float32) * lo_ref[...].astype(jnp.float32), axis=1, keepdims=True
    )
    first = delta.astype(jnp.bfloat16).astype(jnp.float32)
    second = (delta - first).astype(jnp.bfloat16).astype(jnp.float32)
    third = delta - first - second
    pos = start_ref[0] + lax.broadcasted_iota(jnp.int32, (ROWS, 64), 0) // 8
    lane = lax.broadcasted_iota(jnp.int32, (ROWS, 64), 1)
    extra = jnp.where(lane == 0, first, 0.0)
    extra = jnp.where(lane == 1, second, extra)
    extra = jnp.where(lane == 2, third, extra)
    extra = jnp.where(lane == 3, (pos // 64).astype(jnp.float32), extra)
    extra = jnp.where(lane == 4, (pos % 64).astype(jnp.float32), extra)
    out_ref[:, :VALUES] = grad
    out_ref[:, VALUES:VALUES + 512] = q_ref[:, :512]
    out_ref[:, VALUES + 512:] = jnp.concatenate(
        [q_ref[:, 512:576], extra.astype(jnp.bfloat16)], axis=1
    )


def dot_nt(a, b):
    return lax.dot_general(a, b, (((1,), (1,)), ((), ())), preferred_element_type=jnp.float32)


def row_facts(block_ref):
    kind = lax.broadcasted_iota(jnp.int32, (8, 128), 0)
    lane = lax.broadcasted_iota(jnp.int32, (8, 128), 1) - 64
    pick = jnp.where((kind == 0) & (lane >= 0) & (lane <= 2), 1.0, 0.0)
    pick = jnp.where((kind == 1) & (lane == 3), 64.0, pick)
    pick = jnp.where((kind == 1) & (lane == 4), 1.0, pick)
    facts = dot_nt(pick.astype(jnp.bfloat16), block_ref[:, 1024:])
    return facts[0:1], facts[1:2]


def score_kernel(place_ref, lat_ref, x0, x1, x2, x3, p_ref, t_ref, stat_ref):
    blocks = (x0, x1, x2, x3)
    core, odd = place_ref[0] // 2, place_ref[0] % 2
    facts = [row_facts(b) for b in blocks]

    def scores(tile, tops):
        rows = pl.ds(pl.multiple_of(tile * TILE, TILE), TILE)
        n = lax.broadcasted_iota(jnp.int32, (TILE, 1), 0)
        key_pos = (
            (n // 32) * 1024 + (tile // 2) * 256 + core * 128 + (tile % 2) * 64
            + ((n // 8) % 4) * 16 + odd * 8 + n % 8
        ).astype(jnp.float32)
        keys = lat_ref[rows, :]
        new = []
        for k, block in enumerate(blocks):
            s = dot_nt(keys, block[:, VALUES:]) * score_scale
            s = jnp.where(key_pos <= facts[k][1], s, masked_score)
            p_ref[rows, k * ROWS:(k + 1) * ROWS] = s
            new.append(jnp.maximum(tops[k], jnp.max(s, axis=0, keepdims=True)))
        return tuple(new)

    tops = lax.fori_loop(
        0, KEYS // TILE, scores, (jnp.full((1, ROWS), least_top, jnp.float32),) * TEAM
    )

    def weigh(tile, sums):
        rows = pl.ds(pl.multiple_of(tile * TILE, TILE), TILE)
        values = lat_ref[rows, :VALUES]
        new = []
        for k, block in enumerate(blocks):
            cols = slice(k * ROWS, (k + 1) * ROWS)
            p = jnp.exp(p_ref[rows, cols] - tops[k])
            pg = dot_nt(values, block[:, :VALUES])
            p_ref[rows, cols] = p
            t_ref[rows, cols] = p * (pg - facts[k][0])
            new.append(sums[k] + jnp.sum(p, axis=0, keepdims=True))
        return tuple(new)

    sums = lax.fori_loop(
        0, KEYS // TILE, weigh, (jnp.zeros((1, ROWS), jnp.float32),) * TEAM
    )
    stat_ref[...] = jnp.concatenate(tops + sums, axis=0)


def grad_kernel(
    place_ref, own_ref, all_ref, lat_ref, x0, x1, x2, x3, p_ref, t_ref,
    key_ref, near_ref, far_ref, ds_ref,
):
    blocks = (x0, x1, x2, x3)
    place = place_ref[0]
    factors = []
    for k in range(TEAM):
        spots = [place ^ other ^ k for other in range(TEAM)]
        tops = [all_ref[o, pl.ds(spots[o], 1), :] for o in range(TEAM)]
        sums = [all_ref[o, pl.ds(TEAM + spots[o], 1), :] for o in range(TEAM)]
        top = jnp.maximum(jnp.maximum(tops[0], tops[1]), jnp.maximum(tops[2], tops[3]))
        total = sum(z * jnp.exp(m - top) for m, z in zip(tops, sums))
        factors.append(jnp.exp(own_ref[k:k + 1, :] - top) / total)

    def keys(tile, _):
        rows = pl.ds(pl.multiple_of(tile * TILE, TILE), TILE)
        low = high = None
        for k, block in enumerate(blocks):
            cols = slice(k * ROWS, (k + 1) * ROWS)
            w = (p_ref[rows, cols] * factors[k]).astype(jnp.bfloat16)
            ds = (t_ref[rows, cols] * (factors[k] * score_scale)).astype(jnp.bfloat16)
            ds_ref[rows, cols] = ds
            part = jnp.dot(
                ds, block[:, VALUES:VALUES + 512], preferred_element_type=jnp.float32
            ) + jnp.dot(w, block[:, :VALUES], preferred_element_type=jnp.float32)
            tail = jnp.dot(ds, block[:, 1024:], preferred_element_type=jnp.float32)
            low = part if low is None else low + part
            high = tail if high is None else high + tail
        key_ref[rows, :512] = low.astype(key_ref.dtype)
        key_ref[rows, 512:] = high.astype(key_ref.dtype)
        return 0

    lax.fori_loop(0, KEYS // TILE, keys, 0)
    for k in range(TEAM):
        out = lax.dot_general(
            ds_ref[:, k * ROWS:(k + 1) * ROWS], lat_ref[...],
            (((0,), (0,)), ((), ())), preferred_element_type=jnp.float32,
        )
        ref = near_ref if k < 2 else far_ref
        ref[(k % 2) * ROWS:(k % 2 + 1) * ROWS, :] = out[:, :576].astype(ref.dtype)


def whole(n):
    return [pl.BlockSpec(memory_space=pltpu.VMEM)] * n


SMEM = pl.BlockSpec(memory_space=pltpu.SMEM)
LIMIT = pltpu.CompilerParams(vmem_limit_bytes=48 * 1024 * 1024)


def swap(block, axis):
    return lax.ppermute(block, axis, [(0, 1), (1, 0)])


def exchange(pieces, axes):
    return lax.all_to_all(pieces, axes, 0, 0, tiled=True)


def per_device(queries, latents, out_grad, layer_out, query_start):
    place = (lax.axis_index("c") * 2 + lax.axis_index("y0")).astype(jnp.int32).reshape(1)
    head = lax.axis_index(("zl", "yh", "y0"))

    piece = lax.dynamic_slice_in_dim(latents, head * 8, 8, 0)
    piece = jnp.pad(piece, ((0, 0), (0, WIDE - 576)))
    tile = exchange(jnp.broadcast_to(piece[None], (16, 8, WIDE)), ("zh", "yh"))
    tile = tile.reshape(TILE, WIDE)
    lat = exchange(jnp.broadcast_to(tile[None], (8, TILE, WIDE)), ("x", "zl"))
    lat = lat.reshape(KEYS, WIDE)

    x0 = pl.pallas_call(
        prep_kernel,
        out_shape=jax.ShapeDtypeStruct((ROWS, PACK), jnp.bfloat16),
        in_specs=[SMEM] + whole(3),
        out_specs=whole(1)[0],
        name="prep",
    )(
        query_start,
        queries.reshape(ROWS, 576),
        out_grad.reshape(ROWS, VALUES),
        layer_out.reshape(ROWS, VALUES),
    )
    x1 = swap(x0, "y0")
    x2 = swap(x0, "c")
    x3 = swap(x1, "c")

    square = jax.ShapeDtypeStruct((KEYS, TEAM * ROWS), jnp.float32)
    p, t, stats = pl.pallas_call(
        score_kernel,
        out_shape=(square, square, jax.ShapeDtypeStruct((2 * TEAM, ROWS), jnp.float32)),
        in_specs=[SMEM] + whole(5),
        out_specs=tuple(whole(3)),
        compiler_params=LIMIT,
        name="scores",
    )(place, lat, x0, x1, x2, x3)
    team_stats = lax.all_gather(stats, ("c", "y0"), axis=0, tiled=False)

    key_part, near, far = pl.pallas_call(
        grad_kernel,
        out_shape=(
            jax.ShapeDtypeStruct((KEYS, WIDE), jnp.bfloat16),
            jax.ShapeDtypeStruct((2 * ROWS, 576), jnp.float32),
            jax.ShapeDtypeStruct((2 * ROWS, 576), jnp.bfloat16),
        ),
        in_specs=[SMEM] + whole(9),
        out_specs=tuple(whole(3)),
        scratch_shapes=[pltpu.VMEM((KEYS, TEAM * ROWS), jnp.bfloat16)],
        compiler_params=LIMIT,
        name="grads",
    )(place, stats, team_stats, lat, x0, x1, x2, x3, p, t)

    parts = exchange(key_part.reshape(8, TILE, WIDE), ("x", "zl"))
    tile_sum = jnp.sum(parts.astype(jnp.float32), axis=0)
    parts = exchange(tile_sum.reshape(16, 8, WIDE), ("zh", "yh"))
    latent_grad = jnp.sum(parts, axis=0)[:, :576]

    both = near + swap(far, "c").astype(jnp.float32)
    query_sum = both[:ROWS] + swap(both[ROWS:].astype(jnp.bfloat16), "y0").astype(jnp.float32)
    query_grad = query_sum.astype(jnp.bfloat16).reshape(queries.shape)
    return (query_grad, latent_grad)


def solution(mesh):
    fine = Mesh(mesh.devices.reshape(4, 4, 2, 2, 4, 2), FINE)
    seq, head = FINE[:3], FINE[3:]
    placed = (
        P(seq, head, None),
        P(seq, None),
        P(seq, head, None),
        P(seq, head, None),
        P(seq),
    )
    return jax.shard_map(
        per_device,
        mesh=fine,
        in_specs=placed,
        out_specs=(P(seq, head, None), P(FINE, None)),
        check_vma=False,
    )
```

```python
import jax
import jax.numpy as jnp
from jax import lax
from jax.experimental import pallas as pl
from jax.experimental.pallas import tpu as pltpu
from jax.sharding import Mesh, PartitionSpec as P

score_scale = 192 ** (-0.5)
masked_score = -1e30
least_top = -1e29

ROWS = 256
WIDE = 640
VALUES = 512
PACK = 1152
KEYS = 1024
TILE = 256
PIECE = 64
TEAM = 4

FINE = ("zh", "x", "c", "zl", "yh", "y0")


def prep_kernel(start_ref, q_ref, do_ref, lo_ref, out_ref):
    grad = do_ref[...]
    delta = jnp.sum(
        grad.astype(jnp.float32) * lo_ref[...].astype(jnp.float32), axis=1, keepdims=True
    )
    first = delta.astype(jnp.bfloat16).astype(jnp.float32)
    second = (delta - first).astype(jnp.bfloat16).astype(jnp.float32)
    third = delta - first - second
    pos = start_ref[0] + lax.broadcasted_iota(jnp.int32, (ROWS, 64), 0) // 8
    lane = lax.broadcasted_iota(jnp.int32, (ROWS, 64), 1)
    extra = jnp.where(lane == 0, first, 0.0)
    extra = jnp.where(lane == 1, second, extra)
    extra = jnp.where(lane == 2, third, extra)
    extra = jnp.where(lane == 3, (pos // 64).astype(jnp.float32), extra)
    extra = jnp.where(lane == 4, (pos % 64).astype(jnp.float32), extra)
    out_ref[:, :VALUES] = grad
    out_ref[:, VALUES:VALUES + 512] = q_ref[:, :512]
    out_ref[:, VALUES + 512:] = jnp.concatenate(
        [q_ref[:, 512:576], extra.astype(jnp.bfloat16)], axis=1
    )


def dot_nt(a, b):
    return lax.dot_general(a, b, (((1,), (1,)), ((), ())), preferred_element_type=jnp.float32)


def row_facts(block_ref):
    kind = lax.broadcasted_iota(jnp.int32, (8, 128), 0)
    lane = lax.broadcasted_iota(jnp.int32, (8, 128), 1) - 64
    pick = jnp.where((kind == 0) & (lane >= 0) & (lane <= 2), 1.0, 0.0)
    pick = jnp.where((kind == 1) & (lane == 3), 64.0, pick)
    pick = jnp.where((kind == 1) & (lane == 4), 1.0, pick)
    facts = dot_nt(pick.astype(jnp.bfloat16), block_ref[:, 1024:])
    return facts[0:1], facts[1:2]


def spread_kernel(place_ref, lat_ref, out_ref):
    odd = place_ref[0] % 2 == 1
    rows = lat_ref[...].reshape(8, 2, 8, 576)
    mine = jnp.where(odd, rows[:, 1], rows[:, 0]).reshape(PIECE, 576)
    mine = jnp.concatenate([mine, jnp.zeros((PIECE, 64), jnp.bfloat16)], axis=1)
    for peer in range(16):
        out_ref[peer] = mine


def tile_rows(tile):
    return pl.ds(pl.multiple_of(tile * TILE, TILE), TILE)


def block_cols(k):
    return slice(k * ROWS, (k + 1) * ROWS)


def score_kernel(place_ref, lat_ref, x0, x1, x2, x3, p_ref, stat_ref):
    blocks = (x0, x1, x2, x3)
    core, odd = place_ref[0] // 2, place_ref[0] % 2
    poses = [row_facts(b)[1] for b in blocks]

    def scores(tile, tops):
        rows = tile_rows(tile)
        n = lax.broadcasted_iota(jnp.int32, (TILE, 1), 0)
        key_pos = (
            (n // 64) * 1024 + tile * 256 + core * 128 + ((n // 8) % 8) * 16 + odd * 8 + n % 8
        ).astype(jnp.float32)
        keys = lat_ref[rows, :]
        new = []
        for k, block in enumerate(blocks):
            s = dot_nt(keys, block[:, VALUES:]) * score_scale
            s = jnp.where(key_pos <= poses[k], s, masked_score)
            p_ref[rows, block_cols(k)] = s
            new.append(jnp.maximum(tops[k], jnp.max(s, axis=0, keepdims=True)))
        return tuple(new)

    tops = lax.fori_loop(
        0, KEYS // TILE, scores, (jnp.full((1, ROWS), least_top, jnp.float32),) * TEAM
    )

    def weigh(tile, sums):
        rows = tile_rows(tile)
        new = []
        for k in range(TEAM):
            p = jnp.exp(p_ref[rows, block_cols(k)] - tops[k])
            p_ref[rows, block_cols(k)] = p
            new.append(sums[k] + jnp.sum(p, axis=0, keepdims=True))
        return tuple(new)

    sums = lax.fori_loop(
        0, KEYS // TILE, weigh, (jnp.zeros((1, ROWS), jnp.float32),) * TEAM
    )
    stat_ref[...] = jnp.concatenate(tops + sums, axis=0)


def value_kernel(lat_ref, x0, x1, x2, x3, p_ref, t_ref):
    blocks = (x0, x1, x2, x3)
    deltas = [row_facts(b)[0] for b in blocks]

    def values(tile, _):
        rows = tile_rows(tile)
        held = lat_ref[rows, :VALUES]
        for k, block in enumerate(blocks):
            pg = dot_nt(held, block[:, :VALUES])
            t_ref[rows, block_cols(k)] = p_ref[rows, block_cols(k)] * (pg - deltas[k])
        return 0

    lax.fori_loop(0, KEYS // TILE, values, 0)


def key_kernel(
    place_ref, own_ref, here_ref, there_ref, x0, x1, x2, x3, p_ref, t_ref, key_ref, ds_ref
):
    blocks = (x0, x1, x2, x3)
    core = place_ref[0] // 2
    factors = []
    for k in range(TEAM):
        tops, sums = [], []
        for ref, y in ((here_ref, 0), (there_ref, 1)):
            for c in range(2):
                spot = (2 * c + y) ^ k
                tops.append(ref[core ^ c, spot:spot + 1, :])
                sums.append(ref[core ^ c, TEAM + spot:TEAM + spot + 1, :])
        top = jnp.maximum(jnp.maximum(tops[0], tops[1]), jnp.maximum(tops[2], tops[3]))
        total = sum(z * jnp.exp(m - top) for m, z in zip(tops, sums))
        factors.append(jnp.exp(own_ref[k:k + 1, :] - top) / total)

    def keys(tile, _):
        rows = tile_rows(tile)
        low = high = None
        for k, block in enumerate(blocks):
            cols = block_cols(k)
            w = (p_ref[rows, cols] * factors[k]).astype(jnp.bfloat16)
            ds = (t_ref[rows, cols] * (factors[k] * score_scale)).astype(jnp.bfloat16)
            ds_ref[rows, cols] = ds
            part = jnp.dot(
                ds, block[:, VALUES:VALUES + 512], preferred_element_type=jnp.float32
            ) + jnp.dot(w, block[:, :VALUES], preferred_element_type=jnp.float32)
            tail = jnp.dot(ds, block[:, 1024:], preferred_element_type=jnp.float32)
            low = part if low is None else low + part
            high = tail if high is None else high + tail
        both = jnp.concatenate([low, high], axis=1).astype(key_ref.dtype)
        for zl in range(2):
            for zh in range(4):
                key_ref[2 * tile + zl, 32 * zh:32 * zh + 32, :] = both[
                    64 * zh + 32 * zl:64 * zh + 32 * zl + 32
                ]
        return 0

    lax.fori_loop(0, KEYS // TILE, keys, 0)


def query_kernel(lat_ref, ds_ref, near_ref, far_ref):
    for k in range(TEAM):
        out = lax.dot_general(
            ds_ref[:, block_cols(k)], lat_ref[...],
            (((0,), (0,)), ((), ())), preferred_element_type=jnp.float32,
        )
        ref = near_ref if k < 2 else far_ref
        ref[(k % 2) * ROWS:(k % 2 + 1) * ROWS, :] = out.astype(ref.dtype)


def whole(n):
    return [pl.BlockSpec(memory_space=pltpu.VMEM)] * n


SMEM = pl.BlockSpec(memory_space=pltpu.SMEM)


def swap(block, axis):
    return lax.ppermute(block, axis, [(0, 1), (1, 0)])


def exchange(pieces, axes):
    return lax.all_to_all(pieces, axes, 0, 0, tiled=True)


def call(kernel, out_shape, smem, vmem, name, limit=16):
    single = not isinstance(out_shape, tuple)
    return pl.pallas_call(
        kernel,
        out_shape=out_shape,
        in_specs=[SMEM] * smem + whole(vmem),
        out_specs=whole(1)[0] if single else tuple(whole(len(out_shape))),
        compiler_params=pltpu.CompilerParams(vmem_limit_bytes=limit * 1024 * 1024),
        name=name,
    )


def per_device(queries, latents, out_grad, layer_out, query_start):
    place = (lax.axis_index("c") * 2 + lax.axis_index("y0")).astype(jnp.int32).reshape(1)
    shape = jax.ShapeDtypeStruct

    pieces = call(spread_kernel, shape((16, PIECE, WIDE), jnp.bfloat16), 1, 1, "spread")(
        place, latents
    )
    lat = exchange(pieces, ("x", "zh")).reshape(KEYS, WIDE)

    x0 = call(prep_kernel, shape((ROWS, PACK), jnp.bfloat16), 1, 3, "prep")(
        query_start,
        queries.reshape(ROWS, 576),
        out_grad.reshape(ROWS, VALUES),
        layer_out.reshape(ROWS, VALUES),
    )
    x1 = swap(x0, "y0")
    x2 = swap(x0, "c")
    x3 = swap(x1, "c")
    x = (x0, x1, x2, x3)

    square = shape((KEYS, TEAM * ROWS), jnp.float32)
    p, stats = call(
        score_kernel, (square, shape((2 * TEAM, ROWS), jnp.float32)), 1, 5, "scores"
    )(place, lat, *x)
    here = lax.all_gather(stats, "c", axis=0, tiled=False)
    there = swap(here, "y0")
    t = call(value_kernel, square, 0, 6, "values")(lat, *x, p)

    key_part, ds = call(
        key_kernel,
        (
            shape((8, 128, WIDE), jnp.bfloat16),
            shape((KEYS, TEAM * ROWS), jnp.bfloat16),
        ),
        1, 9, "keys",
    )(place, stats, here, there, *x, p, t)
    parts = exchange(key_part, ("x", "zl"))

    near, far = call(
        query_kernel,
        (shape((2 * ROWS, WIDE), jnp.float32), shape((2 * ROWS, WIDE), jnp.bfloat16)),
        0, 2, "query",
    )(lat, ds)
    both = near + swap(far, "c").astype(jnp.float32)
    from_pair = swap(both[ROWS:].astype(jnp.bfloat16), "y0")
    parts, from_pair = lax.optimization_barrier((parts, from_pair))
    query_sum = both[:ROWS] + from_pair.astype(jnp.float32)
    query_grad = query_sum[:, :576].astype(jnp.bfloat16).reshape(queries.shape)

    tile_sum = jnp.sum(parts.astype(jnp.float32), axis=0)
    parts = exchange(tile_sum.reshape(16, 8, WIDE), ("zh", "yh"))
    latent_grad = jnp.sum(parts, axis=0)[:, :576]
    return (query_grad, latent_grad)


def solution(mesh):
    fine = Mesh(mesh.devices.reshape(4, 4, 2, 2, 4, 2), FINE)
    seq, head = FINE[:3], FINE[3:]
    placed = (
        P(seq, head, None),
        P(seq, None),
        P(seq, head, None),
        P(seq, head, None),
        P(seq),
    )
    return jax.shard_map(
        per_device,
        mesh=fine,
        in_specs=placed,
        out_specs=(P(seq, head, None), P(FINE, None)),
        check_vma=False,
    )
```

```python
import jax
import jax.numpy as jnp
from jax import lax
from jax.experimental import pallas as pl
from jax.experimental.pallas import tpu as pltpu
from jax.sharding import Mesh, PartitionSpec as P

score_scale = 192 ** (-0.5)
masked_score = -1e30
least_top = -1e29

ROWS = 256
WIDE = 640
VALUES = 512
PACK = 1152
KEYS = 1024
TILE = 256
PIECE = 64
FOLD = 288
TEAM = 4

FINE = ("zh", "x", "c", "zl", "ya", "yb", "y0")
SIZES = (4, 4, 2, 2, 2, 2, 2)


def prep_kernel(start_ref, q_ref, do_ref, lo_ref, out_ref):
    grad = do_ref[...]
    delta = jnp.sum(
        grad.astype(jnp.float32) * lo_ref[...].astype(jnp.float32), axis=1, keepdims=True
    )
    first = delta.astype(jnp.bfloat16).astype(jnp.float32)
    second = (delta - first).astype(jnp.bfloat16).astype(jnp.float32)
    third = delta - first - second
    pos = start_ref[0] + lax.broadcasted_iota(jnp.int32, (ROWS, 64), 0) // 8
    lane = lax.broadcasted_iota(jnp.int32, (ROWS, 64), 1)
    extra = jnp.where(lane == 0, first, 0.0)
    extra = jnp.where(lane == 1, second, extra)
    extra = jnp.where(lane == 2, third, extra)
    extra = jnp.where(lane == 3, (pos // 64).astype(jnp.float32), extra)
    extra = jnp.where(lane == 4, (pos % 64).astype(jnp.float32), extra)
    out_ref[:, :VALUES] = grad
    out_ref[:, VALUES:VALUES + 512] = q_ref[:, :512]
    out_ref[:, VALUES + 512:] = jnp.concatenate(
        [q_ref[:, 512:576], extra.astype(jnp.bfloat16)], axis=1
    )


def dot_nt(a, b):
    return lax.dot_general(a, b, (((1,), (1,)), ((), ())), preferred_element_type=jnp.float32)


def row_facts(block_ref):
    kind = lax.broadcasted_iota(jnp.int32, (8, 128), 0)
    lane = lax.broadcasted_iota(jnp.int32, (8, 128), 1) - 64
    pick = jnp.where((kind == 0) & (lane >= 0) & (lane <= 2), 1.0, 0.0)
    pick = jnp.where((kind == 1) & (lane == 3), 64.0, pick)
    pick = jnp.where((kind == 1) & (lane == 4), 1.0, pick)
    facts = dot_nt(pick.astype(jnp.bfloat16), block_ref[:, 1024:])
    return facts[0:1], facts[1:2]


def spread_kernel(place_ref, lat_ref, out_ref):
    odd = place_ref[0] % 2 == 1
    rows = lat_ref[...].T.reshape(8, 2, 8, 576)
    mine = jnp.where(odd, rows[:, 1], rows[:, 0]).reshape(PIECE, 576)
    folded = jnp.concatenate(
        [mine[:, 128 * j:128 * j + 128] for j in range(4)]
        + [jnp.concatenate([mine[:32, 512:], mine[32:, 512:]], axis=1)],
        axis=0,
    )
    for peer in range(16):
        out_ref[peer] = folded


def unfold(piece_ref):
    parts = [piece_ref[64 * j:64 * j + 64] for j in range(4)]
    tail = piece_ref[256:288]
    tail = jnp.concatenate([tail[:, :64], tail[:, 64:]], axis=0)
    return jnp.concatenate(parts + [tail, jnp.zeros((PIECE, 64), jnp.bfloat16)], axis=1)


def tile_rows(tile):
    return pl.ds(pl.multiple_of(tile * TILE, TILE), TILE)


def block_cols(k):
    return slice(k * ROWS, (k + 1) * ROWS)


def score_kernel(place_ref, piece_ref, x0, x1, x2, x3, p_ref, stat_ref, lat_ref):
    blocks = (x0, x1, x2, x3)
    core, odd = place_ref[0] // 2, place_ref[0] % 2
    poses = [row_facts(b)[1] for b in blocks]

    def scores(tile, tops):
        rows = tile_rows(tile)
        n = lax.broadcasted_iota(jnp.int32, (TILE, 1), 0)
        key_pos = (
            (n // 64) * 1024 + tile * 256 + core * 128 + ((n // 8) % 8) * 16 + odd * 8 + n % 8
        ).astype(jnp.float32)
        keys = jnp.concatenate([unfold(piece_ref.at[4 * tile + zh]) for zh in range(4)], axis=0)
        lat_ref[rows, :] = keys
        new = []
        for k, block in enumerate(blocks):
            s = dot_nt(keys, block[:, VALUES:]) * score_scale
            s = jnp.where(key_pos <= poses[k], s, masked_score)
            p_ref[rows, block_cols(k)] = s
            new.append(jnp.maximum(tops[k], jnp.max(s, axis=0, keepdims=True)))
        return tuple(new)

    tops = lax.fori_loop(
        0, KEYS // TILE, scores, (jnp.full((1, ROWS), least_top, jnp.float32),) * TEAM
    )

    def weigh(tile, sums):
        rows = tile_rows(tile)
        new = []
        for k in range(TEAM):
            p = jnp.exp(p_ref[rows, block_cols(k)] - tops[k])
            p_ref[rows, block_cols(k)] = p
            new.append(sums[k] + jnp.sum(p, axis=0, keepdims=True))
        return tuple(new)

    sums = lax.fori_loop(
        0, KEYS // TILE, weigh, (jnp.zeros((1, ROWS), jnp.float32),) * TEAM
    )
    stat_ref[...] = jnp.concatenate(tops + sums, axis=0)


def value_kernel(lat_ref, x0, x1, x2, x3, p_ref, t_ref):
    blocks = (x0, x1, x2, x3)
    deltas = [row_facts(b)[0] for b in blocks]

    def values(tile, _):
        rows = tile_rows(tile)
        held = lat_ref[rows, :VALUES]
        for k, block in enumerate(blocks):
            pg = dot_nt(held, block[:, :VALUES])
            t_ref[rows, block_cols(k)] = p_ref[rows, block_cols(k)] * (pg - deltas[k])
        return 0

    lax.fori_loop(0, KEYS // TILE, values, 0)


def row_factors(place_ref, own_ref, team_ref):
    core = place_ref[0] // 2
    factors = []
    for k in range(TEAM):
        tops, sums = [], []
        for y in range(2):
            for c in range(2):
                spot = 8 * y + ((2 * c + y) ^ k)
                tops.append(team_ref[core ^ c, spot:spot + 1, :])
                sums.append(team_ref[core ^ c, TEAM + spot:TEAM + spot + 1, :])
        top = jnp.maximum(jnp.maximum(tops[0], tops[1]), jnp.maximum(tops[2], tops[3]))
        total = sum(z * jnp.exp(m - top) for m, z in zip(tops, sums))
        factors.append(jnp.exp(own_ref[k:k + 1, :] - top) / total)
    return factors


def key_kernel(
    place_ref, own_ref, team_ref, x0, x1, x2, x3, p_ref, t_ref, key_ref, ds_ref,
    held_ref, held_ds, sems,
):
    blocks = (x0, x1, x2, x3)
    factors = row_factors(place_ref, own_ref, team_ref)

    def leave(tile):
        part, rows = pl.ds(tile * 4, 4), tile_rows(tile)
        return (
            pltpu.make_async_copy(held_ref.at[part], key_ref.at[part], sems.at[0, tile]),
            pltpu.make_async_copy(held_ds.at[rows], ds_ref.at[rows], sems.at[1, tile]),
        )

    def keys(tile, _):
        rows = tile_rows(tile)
        low = high = None
        for k, block in enumerate(blocks):
            cols = block_cols(k)
            w = (p_ref[rows, cols] * factors[k]).astype(jnp.bfloat16)
            ds = (t_ref[rows, cols] * (factors[k] * score_scale)).astype(jnp.bfloat16)
            held_ds[rows, cols] = ds
            part = jnp.dot(
                ds, block[:, VALUES:VALUES + 512], preferred_element_type=jnp.float32
            ) + jnp.dot(w, block[:, :VALUES], preferred_element_type=jnp.float32)
            tail = jnp.dot(ds, block[:, 1024:], preferred_element_type=jnp.float32)
            low = part if low is None else low + part
            high = tail if high is None else high + tail
        both = jnp.concatenate([low, high], axis=1)
        for zl in range(2):
            for yb in range(2):
                firsts = [
                    64 * zh + 8 * (4 * zl + 2 * ya + yb) for zh in range(4) for ya in range(2)
                ]
                piece = jnp.concatenate([both[n:n + 8] for n in firsts], axis=0)
                held_ref[4 * tile + 2 * zl + yb] = piece.astype(held_ref.dtype)
        for copy in leave(tile):
            copy.start()
        return 0

    lax.fori_loop(0, KEYS // TILE, keys, 0)
    for tile in range(KEYS // TILE):
        for copy in leave(tile):
            copy.wait()


def query_kernel(lat_ref, ds_ref, near_ref, far_ref):
    for k in range(TEAM):
        out = lax.dot_general(
            ds_ref[:, block_cols(k)], lat_ref[...],
            (((0,), (0,)), ((), ())), preferred_element_type=jnp.float32,
        )
        ref = near_ref if k < 2 else far_ref
        ref[(k % 2) * ROWS:(k % 2 + 1) * ROWS, :] = out.astype(ref.dtype)


def whole(n):
    return [pl.BlockSpec(memory_space=pltpu.VMEM)] * n


SMEM = pl.BlockSpec(memory_space=pltpu.SMEM)


def swap(block, axis):
    return lax.ppermute(block, axis, [(0, 1), (1, 0)])


def exchange(pieces, axes):
    return lax.all_to_all(pieces, axes, 0, 0, tiled=True)


def call(kernel, out_shape, smem, vmem, name, limit=16):
    single = not isinstance(out_shape, tuple)
    return pl.pallas_call(
        kernel,
        out_shape=out_shape,
        in_specs=[SMEM] * smem + whole(vmem),
        out_specs=whole(1)[0] if single else tuple(whole(len(out_shape))),
        compiler_params=pltpu.CompilerParams(vmem_limit_bytes=limit * 1024 * 1024),
        name=name,
    )


def per_device(queries, latents, out_grad, layer_out, query_start):
    place = (lax.axis_index("c") * 2 + lax.axis_index("y0")).astype(jnp.int32).reshape(1)
    shape = jax.ShapeDtypeStruct

    pieces = call(spread_kernel, shape((16, FOLD, 128), jnp.bfloat16), 1, 1, "spread")(
        place, latents.T
    )
    pieces = exchange(pieces, ("x", "zh"))

    x0 = call(prep_kernel, shape((ROWS, PACK), jnp.bfloat16), 1, 3, "prep")(
        query_start,
        queries.reshape(ROWS, 576),
        out_grad.reshape(ROWS, VALUES),
        layer_out.reshape(ROWS, VALUES),
    )
    x1 = swap(x0, "y0")
    x2 = swap(x0, "c")
    x3 = swap(x1, "c")
    x = (x0, x1, x2, x3)

    square = shape((KEYS, TEAM * ROWS), jnp.float32)
    p, stats, lat = call(
        score_kernel,
        (
            square,
            shape((2 * TEAM, ROWS), jnp.float32),
            shape((KEYS, WIDE), jnp.bfloat16),
        ),
        1, 5, "scores",
    )(place, pieces, *x)
    there = swap(stats, "y0")
    t = call(value_kernel, square, 0, 6, "values")(lat, *x, p)
    there, t = lax.optimization_barrier((there, t))
    team = lax.all_gather(jnp.concatenate([stats, there], axis=0), "c", axis=0, tiled=False)

    key_part, ds = pl.pallas_call(
        key_kernel,
        out_shape=(
            pltpu.HBM((16, PIECE, WIDE), jnp.bfloat16),
            pltpu.HBM((KEYS, TEAM * ROWS), jnp.bfloat16),
        ),
        in_specs=[SMEM] + whole(8),
        out_specs=(pl.BlockSpec(memory_space=pltpu.HBM),) * 2,
        scratch_shapes=[
            pltpu.VMEM((16, PIECE, WIDE), jnp.bfloat16),
            pltpu.VMEM((KEYS, TEAM * ROWS), jnp.bfloat16),
            pltpu.SemaphoreType.DMA((2, KEYS // TILE)),
        ],
        compiler_params=pltpu.CompilerParams(vmem_limit_bytes=16 * 1024 * 1024),
        name="keys",
    )(place, stats, team, *x, p, t)
    parts = exchange(key_part, ("x", "zl", "yb"))

    near, far = call(
        query_kernel,
        (shape((2 * ROWS, WIDE), jnp.float32), shape((2 * ROWS, WIDE), jnp.bfloat16)),
        0, 2, "query",
    )(lat, ds)
    both = near + swap(far, "c").astype(jnp.float32)
    from_pair = swap(both[ROWS:].astype(jnp.bfloat16), "y0")
    parts, from_pair = lax.optimization_barrier((parts, from_pair))
    query_sum = both[:ROWS] + from_pair.astype(jnp.float32)
    query_grad = query_sum[:, :576].astype(jnp.bfloat16).reshape(queries.shape)

    tile_sum = jnp.sum(parts.astype(jnp.float32), axis=0)
    parts = exchange(tile_sum.reshape(8, 8, WIDE), ("zh", "ya"))
    latent_grad = jnp.sum(parts, axis=0)[:, :576]
    return (query_grad, latent_grad)


def solution(mesh):
    fine = Mesh(mesh.devices.reshape(SIZES), FINE)
    seq, head = FINE[:3], FINE[3:]
    placed = (
        P(seq, head, None),
        P(seq, None),
        P(seq, head, None),
        P(seq, head, None),
        P(seq),
    )
    return jax.shard_map(
        per_device,
        mesh=fine,
        in_specs=placed,
        out_specs=(P(seq, head, None), P(FINE, None)),
        check_vma=False,
    )
```

```python
import jax
import jax.numpy as jnp
from jax import lax
from jax.experimental import pallas as pl
from jax.experimental.pallas import tpu as pltpu
from jax.sharding import Mesh, PartitionSpec as P

score_scale = 192 ** (-0.5)
masked_score = -1e30
least_top = -1e29

ROWS = 256
WIDE = 640
VALUES = 512
PACK = 1152
KEYS = 1024
TILE = 256
PIECE = 64
FOLD = 288
TEAM = 4

FINE = ("zh", "x", "c", "zl", "yh", "y0")
SIZES = (4, 4, 2, 2, 4, 2)


def prep_kernel(start_ref, q_ref, do_ref, lo_ref, out_ref):
    grad = do_ref[...]
    delta = jnp.sum(
        grad.astype(jnp.float32) * lo_ref[...].astype(jnp.float32), axis=1, keepdims=True
    )
    first = delta.astype(jnp.bfloat16).astype(jnp.float32)
    second = (delta - first).astype(jnp.bfloat16).astype(jnp.float32)
    third = delta - first - second
    pos = start_ref[0] + lax.broadcasted_iota(jnp.int32, (ROWS, 64), 0) // 8
    lane = lax.broadcasted_iota(jnp.int32, (ROWS, 64), 1)
    extra = jnp.where(lane == 0, first, 0.0)
    extra = jnp.where(lane == 1, second, extra)
    extra = jnp.where(lane == 2, third, extra)
    extra = jnp.where(lane == 3, (pos // 64).astype(jnp.float32), extra)
    extra = jnp.where(lane == 4, (pos % 64).astype(jnp.float32), extra)
    out_ref[:, :VALUES] = grad
    out_ref[:, VALUES:VALUES + 512] = q_ref[:, :512]
    out_ref[:, VALUES + 512:] = jnp.concatenate(
        [q_ref[:, 512:576], extra.astype(jnp.bfloat16)], axis=1
    )


def dot_nt(a, b):
    return lax.dot_general(a, b, (((1,), (1,)), ((), ())), preferred_element_type=jnp.float32)


def row_facts(block_ref):
    kind = lax.broadcasted_iota(jnp.int32, (8, 128), 0)
    lane = lax.broadcasted_iota(jnp.int32, (8, 128), 1) - 64
    pick = jnp.where((kind == 0) & (lane >= 0) & (lane <= 2), 1.0, 0.0)
    pick = jnp.where((kind == 1) & (lane == 3), 64.0, pick)
    pick = jnp.where((kind == 1) & (lane == 4), 1.0, pick)
    facts = dot_nt(pick.astype(jnp.bfloat16), block_ref[:, 1024:])
    return facts[0:1], facts[1:2]


def fold(rows):
    return jnp.concatenate(
        [rows[:, 128 * j:128 * j + 128] for j in range(4)]
        + [jnp.concatenate([rows[:32, 512:576], rows[32:, 512:576]], axis=1)],
        axis=0,
    )


def spread_kernel(place_ref, lat_ref, out_ref):
    odd = place_ref[0] % 2 == 1
    rows = lat_ref[...].T.reshape(8, 2, 8, 576)
    mine = jnp.where(odd, rows[:, 1], rows[:, 0]).reshape(PIECE, 576)
    folded = fold(mine)
    for peer in range(16):
        out_ref[peer] = folded


def unfold(piece_ref):
    parts = [piece_ref[64 * j:64 * j + 64] for j in range(4)]
    tail = piece_ref[256:288]
    tail = jnp.concatenate([tail[:, :64], tail[:, 64:]], axis=0)
    return jnp.concatenate(parts + [tail, jnp.zeros((PIECE, 64), jnp.bfloat16)], axis=1)


def tile_rows(tile):
    return pl.ds(pl.multiple_of(tile * TILE, TILE), TILE)


def block_cols(k):
    return slice(k * ROWS, (k + 1) * ROWS)


def score_kernel(place_ref, piece_ref, x0, x1, x2, x3, p_ref, stat_ref, lat_ref):
    blocks = (x0, x1, x2, x3)
    core, odd = place_ref[0] // 2, place_ref[0] % 2
    poses = [row_facts(b)[1] for b in blocks]

    def scores(tile, tops):
        rows = tile_rows(tile)
        n = lax.broadcasted_iota(jnp.int32, (TILE, 1), 0)
        key_pos = (
            (n // 64) * 1024 + tile * 256 + core * 128 + ((n // 8) % 8) * 16 + odd * 8 + n % 8
        ).astype(jnp.float32)
        keys = jnp.concatenate([unfold(piece_ref.at[4 * tile + zh]) for zh in range(4)], axis=0)
        lat_ref[rows, :] = keys
        new = []
        for k, block in enumerate(blocks):
            s = dot_nt(keys, block[:, VALUES:]) * score_scale
            s = jnp.where(key_pos <= poses[k], s, masked_score)
            p_ref[rows, block_cols(k)] = s
            new.append(jnp.maximum(tops[k], jnp.max(s, axis=0, keepdims=True)))
        return tuple(new)

    tops = lax.fori_loop(
        0, KEYS // TILE, scores, (jnp.full((1, ROWS), least_top, jnp.float32),) * TEAM
    )

    def weigh(tile, sums):
        rows = tile_rows(tile)
        new = []
        for k in range(TEAM):
            p = jnp.exp(p_ref[rows, block_cols(k)] - tops[k])
            p_ref[rows, block_cols(k)] = p
            new.append(sums[k] + jnp.sum(p, axis=0, keepdims=True))
        return tuple(new)

    sums = lax.fori_loop(
        0, KEYS // TILE, weigh, (jnp.zeros((1, ROWS), jnp.float32),) * TEAM
    )
    stat_ref[...] = jnp.concatenate(tops + sums, axis=0)


def value_kernel(lat_ref, x0, x1, x2, x3, p_ref, t_ref):
    blocks = (x0, x1, x2, x3)
    deltas = [row_facts(b)[0] for b in blocks]

    def values(tile, _):
        rows = tile_rows(tile)
        held = lat_ref[rows, :VALUES]
        for k, block in enumerate(blocks):
            pg = dot_nt(held, block[:, :VALUES])
            t_ref[rows, block_cols(k)] = p_ref[rows, block_cols(k)] * (pg - deltas[k])
        return 0

    lax.fori_loop(0, KEYS // TILE, values, 0)


def row_factors(place_ref, own_ref, team_ref):
    core = place_ref[0] // 2
    factors = []
    for k in range(TEAM):
        tops, sums = [], []
        for y in range(2):
            for c in range(2):
                spot = 8 * y + ((2 * c + y) ^ k)
                tops.append(team_ref[core ^ c, spot:spot + 1, :])
                sums.append(team_ref[core ^ c, TEAM + spot:TEAM + spot + 1, :])
        top = jnp.maximum(jnp.maximum(tops[0], tops[1]), jnp.maximum(tops[2], tops[3]))
        total = sum(z * jnp.exp(m - top) for m, z in zip(tops, sums))
        factors.append(jnp.exp(own_ref[k:k + 1, :] - top) / total)
    return factors


def key_kernel(
    place_ref, own_ref, team_ref, x0, x1, x2, x3, p_ref, t_ref, key_ref, ds_ref,
    held_ref, held_ds, sems,
):
    blocks = (x0, x1, x2, x3)
    factors = row_factors(place_ref, own_ref, team_ref)

    def leave(tile):
        part, rows = pl.ds(tile * 4, 4), tile_rows(tile)
        return (
            pltpu.make_async_copy(held_ref.at[part], key_ref.at[part], sems.at[0, tile]),
            pltpu.make_async_copy(held_ds.at[rows], ds_ref.at[rows], sems.at[1, tile]),
        )

    def keys(tile, _):
        rows = tile_rows(tile)
        low = high = None
        for k, block in enumerate(blocks):
            cols = block_cols(k)
            w = (p_ref[rows, cols] * factors[k]).astype(jnp.bfloat16)
            ds = (t_ref[rows, cols] * (factors[k] * score_scale)).astype(jnp.bfloat16)
            held_ds[rows, cols] = ds
            part = jnp.dot(
                ds, block[:, VALUES:VALUES + 512], preferred_element_type=jnp.float32
            ) + jnp.dot(w, block[:, :VALUES], preferred_element_type=jnp.float32)
            tail = jnp.dot(ds, block[:, 1024:], preferred_element_type=jnp.float32)
            low = part if low is None else low + part
            high = tail if high is None else high + tail
        both = jnp.concatenate([low, high], axis=1)
        both = both.astype(held_ref.dtype)
        for zh in range(4):
            held_ref[4 * tile + zh] = fold(both[PIECE * zh:PIECE * zh + PIECE])
        for copy in leave(tile):
            copy.start()
        return 0

    lax.fori_loop(0, KEYS // TILE, keys, 0)
    for tile in range(KEYS // TILE):
        for copy in leave(tile):
            copy.wait()


def query_kernel(lat_ref, ds_ref, near_ref, far_ref):
    for k in range(TEAM):
        out = lax.dot_general(
            ds_ref[:, block_cols(k)], lat_ref[...],
            (((0,), (0,)), ((), ())), preferred_element_type=jnp.float32,
        )
        ref = near_ref if k < 2 else far_ref
        ref[(k % 2) * ROWS:(k % 2 + 1) * ROWS, :] = out.astype(ref.dtype)


def sum_kernel(part_ref, out_ref):
    def total(rows):
        return sum(part_ref[peer, rows].astype(jnp.float32) for peer in range(16))

    for j in range(4):
        chunk = total(slice(PIECE * j, PIECE * j + PIECE))
        out_ref[:, 128 * j:128 * j + 128] = chunk.astype(out_ref.dtype)
    tail = total(slice(4 * PIECE, FOLD))
    tail = jnp.concatenate([tail[:, :64], tail[:, 64:]], axis=0)
    tail = jnp.concatenate([tail, jnp.zeros_like(tail)], axis=1)
    out_ref[:, 512:] = tail.astype(out_ref.dtype)


def whole(n):
    return [pl.BlockSpec(memory_space=pltpu.VMEM)] * n


SMEM = pl.BlockSpec(memory_space=pltpu.SMEM)


def swap(block, axis):
    return lax.ppermute(block, axis, [(0, 1), (1, 0)])


def exchange(pieces, axes):
    return lax.all_to_all(pieces, axes, 0, 0, tiled=True)


def call(kernel, out_shape, smem, vmem, name, limit=16):
    single = not isinstance(out_shape, tuple)
    return pl.pallas_call(
        kernel,
        out_shape=out_shape,
        in_specs=[SMEM] * smem + whole(vmem),
        out_specs=whole(1)[0] if single else tuple(whole(len(out_shape))),
        compiler_params=pltpu.CompilerParams(vmem_limit_bytes=limit * 1024 * 1024),
        name=name,
    )


def per_device(queries, latents, out_grad, layer_out, query_start):
    place = (lax.axis_index("c") * 2 + lax.axis_index("y0")).astype(jnp.int32).reshape(1)
    shape = jax.ShapeDtypeStruct

    pieces = call(spread_kernel, shape((16, FOLD, 128), jnp.bfloat16), 1, 1, "spread")(
        place, latents.T
    )
    pieces = exchange(pieces, ("x", "zh"))

    x0 = call(prep_kernel, shape((ROWS, PACK), jnp.bfloat16), 1, 3, "prep")(
        query_start,
        queries.reshape(ROWS, 576),
        out_grad.reshape(ROWS, VALUES),
        layer_out.reshape(ROWS, VALUES),
    )
    x1 = swap(x0, "y0")
    x2 = swap(x0, "c")
    x3 = swap(x1, "c")
    x = (x0, x1, x2, x3)

    square = shape((KEYS, TEAM * ROWS), jnp.float32)
    p, stats, lat = call(
        score_kernel,
        (
            square,
            shape((2 * TEAM, ROWS), jnp.float32),
            shape((KEYS, WIDE), jnp.bfloat16),
        ),
        1, 5, "scores",
    )(place, pieces, *x)
    there = swap(stats, "y0")
    t = call(value_kernel, square, 0, 6, "values")(lat, *x, p)
    there, t = lax.optimization_barrier((there, t))
    team = lax.all_gather(jnp.concatenate([stats, there], axis=0), "c", axis=0, tiled=False)

    key_part, ds = pl.pallas_call(
        key_kernel,
        out_shape=(
            pltpu.HBM((16, FOLD, 128), jnp.bfloat16),
            pltpu.HBM((KEYS, TEAM * ROWS), jnp.bfloat16),
        ),
        in_specs=[SMEM] + whole(8),
        out_specs=(pl.BlockSpec(memory_space=pltpu.HBM),) * 2,
        scratch_shapes=[
            pltpu.VMEM((16, FOLD, 128), jnp.bfloat16),
            pltpu.VMEM((KEYS, TEAM * ROWS), jnp.bfloat16),
            pltpu.SemaphoreType.DMA((2, KEYS // TILE)),
        ],
        compiler_params=pltpu.CompilerParams(vmem_limit_bytes=16 * 1024 * 1024),
        name="keys",
    )(place, stats, team, *x, p, t)
    parts = exchange(key_part, ("x", "zh"))

    near, far = call(
        query_kernel,
        (shape((2 * ROWS, WIDE), jnp.float32), shape((2 * ROWS, WIDE), jnp.bfloat16)),
        0, 2, "query",
    )(lat, ds)
    both = near + swap(far, "c").astype(jnp.float32)
    from_pair = swap(both[ROWS:].astype(jnp.bfloat16), "y0")
    parts, from_pair = lax.optimization_barrier((parts, from_pair))
    query_sum = both[:ROWS] + from_pair.astype(jnp.float32)
    query_grad = query_sum[:, :576].astype(jnp.bfloat16).reshape(queries.shape)

    tile_sum = call(sum_kernel, shape((PIECE, WIDE), jnp.bfloat16), 0, 1, "sum")(parts)
    parts = exchange(tile_sum.reshape(8, 8, WIDE), ("zl", "yh"))
    latent_grad = jnp.sum(parts.astype(jnp.float32), axis=0)[:, :576]
    return (query_grad, latent_grad)


def solution(mesh):
    fine = Mesh(mesh.devices.reshape(SIZES), FINE)
    seq, head = FINE[:3], FINE[3:]
    placed = (
        P(seq, head, None),
        P(seq, None),
        P(seq, head, None),
        P(seq, head, None),
        P(seq),
    )
    return jax.shard_map(
        per_device,
        mesh=fine,
        in_specs=placed,
        out_specs=(P(seq, head, None), P(FINE, None)),
        check_vma=False,
    )
```

```python
import jax
import jax.numpy as jnp
from jax import lax
from jax.experimental import pallas as pl
from jax.experimental.pallas import tpu as pltpu
from jax.sharding import Mesh, PartitionSpec as P

score_scale = 192 ** (-0.5)
masked_score = -1e30
least_top = -1e29

ROWS = 256
WIDE = 640
VALUES = 512
PACK = 1152
KEYS = 1024
TILE = 256
PIECE = 64
FOLD = 288
TEAM = 4

FINE = ("zh", "x", "c", "zl", "yh", "y0")
SIZES = (4, 4, 2, 2, 4, 2)


def prep_kernel(start_ref, q_ref, do_ref, lo_ref, out_ref):
    grad = do_ref[...]
    delta = jnp.sum(
        grad.astype(jnp.float32) * lo_ref[...].astype(jnp.float32), axis=1, keepdims=True
    )
    first = delta.astype(jnp.bfloat16).astype(jnp.float32)
    second = (delta - first).astype(jnp.bfloat16).astype(jnp.float32)
    third = delta - first - second
    pos = start_ref[0] + lax.broadcasted_iota(jnp.int32, (ROWS, 64), 0) // 8
    lane = lax.broadcasted_iota(jnp.int32, (ROWS, 64), 1)
    extra = jnp.where(lane == 0, first, 0.0)
    extra = jnp.where(lane == 1, second, extra)
    extra = jnp.where(lane == 2, third, extra)
    extra = jnp.where(lane == 3, (pos // 64).astype(jnp.float32), extra)
    extra = jnp.where(lane == 4, (pos % 64).astype(jnp.float32), extra)
    out_ref[:, :VALUES] = grad
    out_ref[:, VALUES:VALUES + 512] = q_ref[:, :512]
    out_ref[:, VALUES + 512:] = jnp.concatenate(
        [q_ref[:, 512:576], extra.astype(jnp.bfloat16)], axis=1
    )


def dot_nt(a, b):
    return lax.dot_general(a, b, (((1,), (1,)), ((), ())), preferred_element_type=jnp.float32)


def row_facts(block_ref):
    kind = lax.broadcasted_iota(jnp.int32, (8, 128), 0)
    lane = lax.broadcasted_iota(jnp.int32, (8, 128), 1) - 64
    pick = jnp.where((kind == 0) & (lane >= 0) & (lane <= 2), 1.0, 0.0)
    pick = jnp.where((kind == 1) & (lane == 3), 64.0, pick)
    pick = jnp.where((kind == 1) & (lane == 4), 1.0, pick)
    facts = dot_nt(pick.astype(jnp.bfloat16), block_ref[:, 1024:])
    return facts[0:1], facts[1:2]


def spread_kernel(place_ref, lat_ref, out_ref):
    odd = place_ref[0] % 2 == 1
    rows = lat_ref[...].T.reshape(8, 2, 8, 576)
    mine = jnp.where(odd, rows[:, 1], rows[:, 0]).reshape(PIECE, 576)
    folded = jnp.concatenate(
        [mine[:, 128 * j:128 * j + 128] for j in range(4)]
        + [jnp.concatenate([mine[:32, 512:], mine[32:, 512:]], axis=1)],
        axis=0,
    )
    for peer in range(16):
        out_ref[peer] = folded


def unfold(piece_ref):
    parts = [piece_ref[64 * j:64 * j + 64] for j in range(4)]
    tail = piece_ref[256:288]
    tail = jnp.concatenate([tail[:, :64], tail[:, 64:]], axis=0)
    return jnp.concatenate(parts + [tail, jnp.zeros((PIECE, 64), jnp.bfloat16)], axis=1)


def tile_rows(tile):
    return pl.ds(pl.multiple_of(tile * TILE, TILE), TILE)


def block_cols(k):
    return slice(k * ROWS, (k + 1) * ROWS)


def score_kernel(place_ref, piece_ref, x0, x1, x2, x3, p_ref, stat_ref, lat_ref):
    blocks = (x0, x1, x2, x3)
    core, odd = place_ref[0] // 2, place_ref[0] % 2
    poses = [row_facts(b)[1] for b in blocks]

    def scores(tile, tops):
        rows = tile_rows(tile)
        n = lax.broadcasted_iota(jnp.int32, (TILE, 1), 0)
        key_pos = (
            (n // 64) * 1024 + tile * 256 + core * 128 + ((n // 8) % 8) * 16 + odd * 8 + n % 8
        ).astype(jnp.float32)
        keys = jnp.concatenate([unfold(piece_ref.at[4 * tile + zh]) for zh in range(4)], axis=0)
        lat_ref[rows, :] = keys
        new = []
        for k, block in enumerate(blocks):
            s = dot_nt(keys, block[:, VALUES:]) * score_scale
            s = jnp.where(key_pos <= poses[k], s, masked_score)
            p_ref[rows, block_cols(k)] = s
            new.append(jnp.maximum(tops[k], jnp.max(s, axis=0, keepdims=True)))
        return tuple(new)

    tops = lax.fori_loop(
        0, KEYS // TILE, scores, (jnp.full((1, ROWS), least_top, jnp.float32),) * TEAM
    )

    def weigh(tile, sums):
        rows = tile_rows(tile)
        new = []
        for k in range(TEAM):
            p = jnp.exp(p_ref[rows, block_cols(k)] - tops[k])
            p_ref[rows, block_cols(k)] = p
            new.append(sums[k] + jnp.sum(p, axis=0, keepdims=True))
        return tuple(new)

    sums = lax.fori_loop(
        0, KEYS // TILE, weigh, (jnp.zeros((1, ROWS), jnp.float32),) * TEAM
    )
    stat_ref[...] = jnp.concatenate(tops + sums, axis=0)


def value_kernel(lat_ref, x0, x1, x2, x3, p_ref, t_ref):
    blocks = (x0, x1, x2, x3)
    deltas = [row_facts(b)[0] for b in blocks]

    def values(tile, _):
        rows = tile_rows(tile)
        held = lat_ref[rows, :VALUES]
        for k, block in enumerate(blocks):
            pg = dot_nt(held, block[:, :VALUES])
            t_ref[rows, block_cols(k)] = p_ref[rows, block_cols(k)] * (pg - deltas[k])
        return 0

    lax.fori_loop(0, KEYS // TILE, values, 0)


def row_factors(place_ref, own_ref, team_ref):
    core = place_ref[0] // 2
    factors = []
    for k in range(TEAM):
        tops, sums = [], []
        for y in range(2):
            for c in range(2):
                spot = 8 * y + ((2 * c + y) ^ k)
                tops.append(team_ref[core ^ c, spot:spot + 1, :])
                sums.append(team_ref[core ^ c, TEAM + spot:TEAM + spot + 1, :])
        top = jnp.maximum(jnp.maximum(tops[0], tops[1]), jnp.maximum(tops[2], tops[3]))
        total = sum(z * jnp.exp(m - top) for m, z in zip(tops, sums))
        factors.append(jnp.exp(own_ref[k:k + 1, :] - top) / total)
    return factors


def key_kernel(
    place_ref, own_ref, team_ref, x0, x1, x2, x3, p_ref, t_ref, key_ref, ds_ref,
    held_ref, held_ds, sems,
):
    blocks = (x0, x1, x2, x3)
    factors = row_factors(place_ref, own_ref, team_ref)

    def leave(tile):
        part, rows = pl.ds(tile * 2, 2), tile_rows(tile)
        return (
            pltpu.make_async_copy(held_ref.at[part], key_ref.at[part], sems.at[0, tile]),
            pltpu.make_async_copy(held_ds.at[rows], ds_ref.at[rows], sems.at[1, tile]),
        )

    def keys(tile, _):
        rows = tile_rows(tile)
        low = high = None
        for k, block in enumerate(blocks):
            cols = block_cols(k)
            w = (p_ref[rows, cols] * factors[k]).astype(jnp.bfloat16)
            ds = (t_ref[rows, cols] * (factors[k] * score_scale)).astype(jnp.bfloat16)
            held_ds[rows, cols] = ds
            part = jnp.dot(
                ds, block[:, VALUES:VALUES + 512], preferred_element_type=jnp.float32
            ) + jnp.dot(w, block[:, :VALUES], preferred_element_type=jnp.float32)
            tail = jnp.dot(ds, block[:, 1024:], preferred_element_type=jnp.float32)
            low = part if low is None else low + part
            high = tail if high is None else high + tail
        both = jnp.concatenate([low, high], axis=1)
        for zl in range(2):
            part = jnp.concatenate(
                [both[n:n + 32] for n in range(32 * zl, TILE, 64)], axis=0
            ).astype(held_ref.dtype)
            for j in range(4):
                held_ref[2 * tile + zl, 128 * j:128 * j + 128] = part[:, 128 * j:128 * j + 128]
            held_ref[2 * tile + zl, 512:] = jnp.concatenate(
                [part[:64, 512:576], part[64:, 512:576]], axis=1
            )
        for copy in leave(tile):
            copy.start()
        return 0

    lax.fori_loop(0, KEYS // TILE, keys, 0)
    for tile in range(KEYS // TILE):
        for copy in leave(tile):
            copy.wait()


def query_kernel(lat_ref, ds_ref, near_ref, far_ref, held_ref, sems):
    def bring(k):
        return pltpu.make_async_copy(ds_ref.at[:, block_cols(k)], held_ref.at[k], sems.at[k])

    for k in range(TEAM):
        bring(k).start()
    for k in (2, 3, 0, 1):
        bring(k).wait()
        out = lax.dot_general(
            held_ref[k], lat_ref[...],
            (((0,), (0,)), ((), ())), preferred_element_type=jnp.float32,
        )
        ref = near_ref if k < 2 else far_ref
        ref[(k % 2) * ROWS:(k % 2 + 1) * ROWS, :] = out.astype(ref.dtype)


def sum_kernel(part_ref, out_ref):
    def total(rows):
        return sum(part_ref[peer, rows].astype(jnp.float32) for peer in range(8))

    for j in range(4):
        chunk = total(slice(128 * j, 128 * j + 128))
        out_ref[:, 128 * j:128 * j + 128] = chunk.astype(out_ref.dtype)
    tail = total(slice(512, 576))
    tail = jnp.concatenate([tail[:, :64], tail[:, 64:]], axis=0)
    tail = jnp.concatenate([tail, jnp.zeros_like(tail)], axis=1)
    out_ref[:, 512:] = tail.astype(out_ref.dtype)


def whole(n):
    return [pl.BlockSpec(memory_space=pltpu.VMEM)] * n


SMEM = pl.BlockSpec(memory_space=pltpu.SMEM)


def swap(block, axis):
    return lax.ppermute(block, axis, [(0, 1), (1, 0)])


def exchange(pieces, axes):
    return lax.all_to_all(pieces, axes, 0, 0, tiled=True)


def call(kernel, out_shape, smem, vmem, name, limit=16):
    single = not isinstance(out_shape, tuple)
    return pl.pallas_call(
        kernel,
        out_shape=out_shape,
        in_specs=[SMEM] * smem + whole(vmem),
        out_specs=whole(1)[0] if single else tuple(whole(len(out_shape))),
        compiler_params=pltpu.CompilerParams(vmem_limit_bytes=limit * 1024 * 1024),
        name=name,
    )


def per_device(queries, latents, out_grad, layer_out, query_start):
    place = (lax.axis_index("c") * 2 + lax.axis_index("y0")).astype(jnp.int32).reshape(1)
    shape = jax.ShapeDtypeStruct

    pieces = call(spread_kernel, shape((16, FOLD, 128), jnp.bfloat16), 1, 1, "spread")(
        place, latents.T
    )
    pieces = exchange(pieces, ("x", "zh"))

    x0 = call(prep_kernel, shape((ROWS, PACK), jnp.bfloat16), 1, 3, "prep")(
        query_start,
        queries.reshape(ROWS, 576),
        out_grad.reshape(ROWS, VALUES),
        layer_out.reshape(ROWS, VALUES),
    )
    x1 = swap(x0, "y0")
    x2 = swap(x0, "c")
    x3 = swap(x1, "c")
    x = (x0, x1, x2, x3)

    square = shape((KEYS, TEAM * ROWS), jnp.float32)
    p, stats, lat = call(
        score_kernel,
        (
            square,
            shape((2 * TEAM, ROWS), jnp.float32),
            shape((KEYS, WIDE), jnp.bfloat16),
        ),
        1, 5, "scores",
    )(place, pieces, *x)
    there = swap(stats, "y0")
    t = call(value_kernel, square, 0, 6, "values")(lat, *x, p)
    there, t = lax.optimization_barrier((there, t))
    team = lax.all_gather(jnp.concatenate([stats, there], axis=0), "c", axis=0, tiled=False)

    key_part, ds = pl.pallas_call(
        key_kernel,
        out_shape=(
            pltpu.HBM((8, 576, 128), jnp.bfloat16),
            pltpu.HBM((KEYS, TEAM * ROWS), jnp.bfloat16),
        ),
        in_specs=[SMEM] + whole(8),
        out_specs=(pl.BlockSpec(memory_space=pltpu.HBM),) * 2,
        scratch_shapes=[
            pltpu.VMEM((8, 576, 128), jnp.bfloat16),
            pltpu.VMEM((KEYS, TEAM * ROWS), jnp.bfloat16),
            pltpu.SemaphoreType.DMA((2, KEYS // TILE)),
        ],
        compiler_params=pltpu.CompilerParams(vmem_limit_bytes=16 * 1024 * 1024),
        name="keys",
    )(place, stats, team, *x, p, t)
    parts = exchange(key_part, ("x", "zl"))

    near, far = pl.pallas_call(
        query_kernel,
        out_shape=(
            shape((2 * ROWS, WIDE), jnp.float32),
            shape((2 * ROWS, WIDE), jnp.bfloat16),
        ),
        in_specs=whole(1) + [pl.BlockSpec(memory_space=pltpu.HBM)],
        out_specs=tuple(whole(2)),
        scratch_shapes=[
            pltpu.VMEM((TEAM, KEYS, ROWS), jnp.bfloat16),
            pltpu.SemaphoreType.DMA((TEAM,)),
        ],
        compiler_params=pltpu.CompilerParams(vmem_limit_bytes=16 * 1024 * 1024),
        name="query",
    )(lat, pltpu.with_memory_space_constraint(ds, pltpu.HBM))
    both = near + swap(far, "c").astype(jnp.float32)
    for_pair = both[ROWS:].astype(jnp.bfloat16)
    parts, for_pair = lax.optimization_barrier((parts, for_pair))
    from_pair = swap(for_pair, "y0")
    query_sum = both[:ROWS] + from_pair.astype(jnp.float32)
    query_grad = query_sum[:, :576].astype(jnp.bfloat16).reshape(queries.shape)

    tile_sum = call(sum_kernel, shape((128, WIDE), jnp.bfloat16), 0, 1, "sum")(parts)
    parts = exchange(tile_sum.reshape(16, 8, WIDE), ("zh", "yh"))
    latent_grad = jnp.sum(parts.astype(jnp.float32), axis=0)[:, :576]
    return (query_grad, latent_grad)


def solution(mesh):
    fine = Mesh(mesh.devices.reshape(SIZES), FINE)
    seq, head = FINE[:3], FINE[3:]
    placed = (
        P(seq, head, None),
        P(seq, None),
        P(seq, head, None),
        P(seq, head, None),
        P(seq),
    )
    return jax.shard_map(
        per_device,
        mesh=fine,
        in_specs=placed,
        out_specs=(P(seq, head, None), P(FINE, None)),
        check_vma=False,
    )
```

```python
import jax
import jax.numpy as jnp
from jax import lax
from jax.experimental import pallas as pl
from jax.experimental.pallas import tpu as pltpu
from jax.sharding import Mesh, PartitionSpec as P

score_scale = 192 ** (-0.5)
masked_score = -1e30
least_top = -1e29

ROWS = 256
WIDE = 640
VALUES = 512
PACK = 1152
KEYS = 1024
TILE = 256
PIECE = 64
FOLD = 288
TEAM = 4
TILES = KEYS // TILE

FINE = ("zh", "x", "c", "zl", "yh", "y0")
SIZES = (4, 4, 2, 2, 4, 2)


def prep_kernel(start_ref, q_ref, do_ref, lo_ref, out_ref):
    grad = do_ref[...]
    delta = jnp.sum(
        grad.astype(jnp.float32) * lo_ref[...].astype(jnp.float32), axis=1, keepdims=True
    )
    first = delta.astype(jnp.bfloat16).astype(jnp.float32)
    second = (delta - first).astype(jnp.bfloat16).astype(jnp.float32)
    third = delta - first - second
    pos = start_ref[0] + lax.broadcasted_iota(jnp.int32, (ROWS, 64), 0) // 8
    lane = lax.broadcasted_iota(jnp.int32, (ROWS, 64), 1)
    extra = jnp.where(lane == 0, first, 0.0)
    extra = jnp.where(lane == 1, second, extra)
    extra = jnp.where(lane == 2, third, extra)
    extra = jnp.where(lane == 3, (pos // 64).astype(jnp.float32), extra)
    extra = jnp.where(lane == 4, (pos % 64).astype(jnp.float32), extra)
    out_ref[:, :VALUES] = grad
    out_ref[:, VALUES:VALUES + 512] = q_ref[:, :512]
    out_ref[:, VALUES + 512:] = jnp.concatenate(
        [q_ref[:, 512:576], extra.astype(jnp.bfloat16)], axis=1
    )


def dot_nt(a, b):
    return lax.dot_general(a, b, (((1,), (1,)), ((), ())), preferred_element_type=jnp.float32)


def row_facts(block_ref):
    kind = lax.broadcasted_iota(jnp.int32, (8, 128), 0)
    lane = lax.broadcasted_iota(jnp.int32, (8, 128), 1) - 64
    pick = jnp.where((kind == 0) & (lane >= 0) & (lane <= 2), 1.0, 0.0)
    pick = jnp.where((kind == 1) & (lane == 3), 64.0, pick)
    pick = jnp.where((kind == 1) & (lane == 4), 1.0, pick)
    facts = dot_nt(pick.astype(jnp.bfloat16), block_ref[:, 1024:])
    return facts[0:1], facts[1:2]


def spread_kernel(place_ref, lat_ref, out_ref):
    odd = place_ref[0] % 2 == 1
    rows = lat_ref[...].T.reshape(8, 2, 8, 576)
    mine = jnp.where(odd, rows[:, 1], rows[:, 0]).reshape(PIECE, 576)
    folded = jnp.concatenate(
        [mine[:, 128 * j:128 * j + 128] for j in range(4)]
        + [jnp.concatenate([mine[:32, 512:], mine[32:, 512:]], axis=1)],
        axis=0,
    )
    for peer in range(4):
        out_ref[peer] = folded


def unfold(piece_ref):
    parts = [piece_ref[64 * j:64 * j + 64] for j in range(4)]
    tail = piece_ref[256:288]
    tail = jnp.concatenate([tail[:, :64], tail[:, 64:]], axis=0)
    return jnp.concatenate(parts + [tail, jnp.zeros((PIECE, 64), jnp.bfloat16)], axis=1)


def tile_rows(tile):
    return pl.ds(pl.multiple_of(tile * TILE, TILE), TILE)


def block_cols(k):
    return slice(k * ROWS, (k + 1) * ROWS)


def score_kernel(place_ref, piece_ref, x0, x1, x2, x3, p_ref, stat_ref, lat_ref, top_ref):
    blocks = (x0, x1, x2, x3)
    core, odd = place_ref[0] // 2, place_ref[0] % 2
    poses = [row_facts(b)[1] for b in blocks]

    tops, sums = [], []
    for tile in range(TILES):
        rows = slice(tile * TILE, tile * TILE + TILE)
        n = lax.broadcasted_iota(jnp.int32, (TILE, 1), 0)
        key_pos = (
            (n // 64) * 1024 + tile * 256 + core * 128 + ((n // 8) % 8) * 16 + odd * 8 + n % 8
        ).astype(jnp.float32)
        keys = jnp.concatenate([unfold(piece_ref.at[4 * tile + zh]) for zh in range(4)], axis=0)
        lat_ref[rows, :] = keys
        for k, block in enumerate(blocks):
            s = dot_nt(keys, block[:, VALUES:]) * score_scale
            s = jnp.where(key_pos <= poses[k], s, masked_score)
            top = jnp.maximum(jnp.max(s, axis=0, keepdims=True), least_top)
            p = jnp.exp(s - top)
            p_ref[rows, block_cols(k)] = p
            tops.append(top)
            sums.append(jnp.sum(p, axis=0, keepdims=True))
    all_tops, all_sums = [], []
    for k in range(TEAM):
        top = tops[k]
        for tile in range(1, TILES):
            top = jnp.maximum(top, tops[TEAM * tile + k])
        all_tops.append(top)
        all_sums.append(
            sum(
                sums[TEAM * tile + k] * jnp.exp(tops[TEAM * tile + k] - top)
                for tile in range(TILES)
            )
        )
    top_ref[...] = jnp.concatenate(tops, axis=0)
    stat_ref[...] = jnp.concatenate(all_tops + all_sums, axis=0)


def value_kernel(lat_ref, x0, x1, x2, x3, p_ref, t_ref):
    blocks = (x0, x1, x2, x3)
    deltas = [row_facts(b)[0] for b in blocks]

    def values(tile, _):
        rows = tile_rows(tile)
        held = lat_ref[rows, :VALUES]
        for k, block in enumerate(blocks):
            pg = dot_nt(held, block[:, :VALUES])
            t_ref[rows, block_cols(k)] = p_ref[rows, block_cols(k)] * (pg - deltas[k])
        return 0

    lax.fori_loop(0, KEYS // TILE, values, 0, unroll=True)


def row_factors(place_ref, own_ref, team_ref):
    core = place_ref[0] // 2
    factors = []
    for k in range(TEAM):
        tops, sums = [], []
        for y in range(2):
            for c in range(2):
                spot = 8 * y + ((2 * c + y) ^ k)
                tops.append(team_ref[core ^ c, spot:spot + 1, :])
                sums.append(team_ref[core ^ c, TEAM + spot:TEAM + spot + 1, :])
        top = jnp.maximum(jnp.maximum(tops[0], tops[1]), jnp.maximum(tops[2], tops[3]))
        total = sum(z * jnp.exp(m - top) for m, z in zip(tops, sums))
        inverse = 1.0 / total
        factors.append(
            [
                jnp.exp(own_ref[TEAM * t + k:TEAM * t + k + 1, :] - top) * inverse
                for t in range(TILES)
            ]
        )
    return factors


def key_kernel(
    place_ref, own_ref, team_ref, x0, x1, x2, x3, p_ref, t_ref, key_ref, ds_ref,
    held_ref, held_ds, sems,
):
    blocks = (x0, x1, x2, x3)
    factors = row_factors(place_ref, own_ref, team_ref)

    def leave(tile):
        part, rows = pl.ds(tile * 2, 2), tile_rows(tile)
        return (
            pltpu.make_async_copy(held_ref.at[part], key_ref.at[part], sems.at[0, tile]),
            pltpu.make_async_copy(held_ds.at[rows], ds_ref.at[rows], sems.at[1, tile]),
        )

    for tile in range(TILES):
        rows = slice(tile * TILE, tile * TILE + TILE)
        low = high = None
        for k, block in enumerate(blocks):
            cols = block_cols(k)
            w = (p_ref[rows, cols] * factors[k][tile]).astype(jnp.bfloat16)
            ds = (t_ref[rows, cols] * (factors[k][tile] * score_scale)).astype(jnp.bfloat16)
            held_ds[rows, cols] = ds
            part = jnp.dot(
                ds, block[:, VALUES:VALUES + 512], preferred_element_type=jnp.float32
            ) + jnp.dot(w, block[:, :VALUES], preferred_element_type=jnp.float32)
            tail = jnp.dot(ds, block[:, 1024:], preferred_element_type=jnp.float32)
            low = part if low is None else low + part
            high = tail if high is None else high + tail
        both = jnp.concatenate([low, high], axis=1)
        for zl in range(2):
            part = jnp.concatenate(
                [both[n:n + 32] for n in range(32 * zl, TILE, 64)], axis=0
            ).astype(held_ref.dtype)
            for j in range(4):
                held_ref[2 * tile + zl, 128 * j:128 * j + 128] = part[:, 128 * j:128 * j + 128]
            held_ref[2 * tile + zl, 512:] = jnp.concatenate(
                [part[:64, 512:576], part[64:, 512:576]], axis=1
            )
        for copy in leave(tile):
            copy.start()
    for tile in range(KEYS // TILE):
        for copy in leave(tile):
            copy.wait()


def query_kernel(lat_ref, ds_ref, near_ref, far_ref, held_ref, sems):
    def bring(k):
        return pltpu.make_async_copy(ds_ref.at[:, block_cols(k)], held_ref.at[k], sems.at[k])

    for k in range(TEAM):
        bring(k).start()
    for k in (2, 3, 0, 1):
        bring(k).wait()
        out = lax.dot_general(
            held_ref[k], lat_ref[...],
            (((0,), (0,)), ((), ())), preferred_element_type=jnp.float32,
        )
        ref = near_ref if k < 2 else far_ref
        ref[(k % 2) * ROWS:(k % 2 + 1) * ROWS, :] = out.astype(ref.dtype)


def sum_kernel(part_ref, out_ref):
    def total(rows):
        return sum(part_ref[peer, rows].astype(jnp.float32) for peer in range(8))

    for j in range(4):
        chunk = total(slice(128 * j, 128 * j + 128))
        out_ref[:, 128 * j:128 * j + 128] = chunk.astype(out_ref.dtype)
    tail = total(slice(512, 576))
    tail = jnp.concatenate([tail[:, :64], tail[:, 64:]], axis=0)
    tail = jnp.concatenate([tail, jnp.zeros_like(tail)], axis=1)
    out_ref[:, 512:] = tail.astype(out_ref.dtype)


def copy_kernel(rows_ref, out_ref, sems):
    copies = [
        pltpu.make_async_copy(rows_ref, out_ref.at[peer], sems.at[peer]) for peer in range(4)
    ]
    for copy in copies:
        copy.start()
    for copy in copies:
        copy.wait()


def whole(n):
    return [pl.BlockSpec(memory_space=pltpu.VMEM)] * n


SMEM = pl.BlockSpec(memory_space=pltpu.SMEM)


def swap(block, axis):
    return lax.ppermute(block, axis, [(0, 1), (1, 0)])


def exchange(pieces, axes):
    return lax.all_to_all(pieces, axes, 0, 0, tiled=True)


def call(kernel, out_shape, smem, vmem, name, limit=16):
    single = not isinstance(out_shape, tuple)
    return pl.pallas_call(
        kernel,
        out_shape=out_shape,
        in_specs=[SMEM] * smem + whole(vmem),
        out_specs=whole(1)[0] if single else tuple(whole(len(out_shape))),
        compiler_params=pltpu.CompilerParams(vmem_limit_bytes=limit * 1024 * 1024),
        name=name,
    )


def per_device(queries, latents, out_grad, layer_out, query_start):
    place = (lax.axis_index("c") * 2 + lax.axis_index("y0")).astype(jnp.int32).reshape(1)
    shape = jax.ShapeDtypeStruct

    pieces = call(spread_kernel, shape((4, FOLD, 128), jnp.bfloat16), 1, 1, "spread")(
        place, latents.T
    )
    pieces = exchange(pieces, ("zh",))
    pieces = pl.pallas_call(
        copy_kernel,
        out_shape=pltpu.HBM((4, 4, FOLD, 128), jnp.bfloat16),
        in_specs=whole(1),
        out_specs=pl.BlockSpec(memory_space=pltpu.HBM),
        scratch_shapes=[pltpu.SemaphoreType.DMA((4,))],
        compiler_params=pltpu.CompilerParams(vmem_limit_bytes=16 * 1024 * 1024),
        name="copies",
    )(pieces)
    pieces = exchange(pieces, ("x",))
    pieces = pieces.reshape(16, FOLD, 128)

    x0 = call(prep_kernel, shape((ROWS, PACK), jnp.bfloat16), 1, 3, "prep")(
        query_start,
        queries.reshape(ROWS, 576),
        out_grad.reshape(ROWS, VALUES),
        layer_out.reshape(ROWS, VALUES),
    )
    x1 = swap(x0, "y0")
    x2 = swap(x0, "c")
    x3 = swap(x1, "c")
    x = (x0, x1, x2, x3)

    square = shape((KEYS, TEAM * ROWS), jnp.float32)
    p, stats, lat, tops = call(
        score_kernel,
        (
            square,
            shape((2 * TEAM, ROWS), jnp.float32),
            shape((KEYS, WIDE), jnp.bfloat16),
            shape((TILES * TEAM, ROWS), jnp.float32),
        ),
        1, 5, "scores",
    )(place, pieces, *x)
    there = swap(stats, "y0")
    t = call(value_kernel, square, 0, 6, "values")(lat, *x, p)
    there, t = lax.optimization_barrier((there, t))
    team = lax.all_gather(jnp.concatenate([stats, there], axis=0), "c", axis=0, tiled=False)

    key_part, ds = pl.pallas_call(
        key_kernel,
        out_shape=(
            pltpu.HBM((8, 576, 128), jnp.bfloat16),
            pltpu.HBM((KEYS, TEAM * ROWS), jnp.bfloat16),
        ),
        in_specs=[SMEM] + whole(8),
        out_specs=(pl.BlockSpec(memory_space=pltpu.HBM),) * 2,
        scratch_shapes=[
            pltpu.VMEM((8, 576, 128), jnp.bfloat16),
            pltpu.VMEM((KEYS, TEAM * ROWS), jnp.bfloat16),
            pltpu.SemaphoreType.DMA((2, KEYS // TILE)),
        ],
        compiler_params=pltpu.CompilerParams(vmem_limit_bytes=16 * 1024 * 1024),
        name="keys",
    )(place, tops, team, *x, p, t)
    parts = exchange(key_part, ("x", "zl"))

    near, far = pl.pallas_call(
        query_kernel,
        out_shape=(
            shape((2 * ROWS, WIDE), jnp.float32),
            shape((2 * ROWS, WIDE), jnp.bfloat16),
        ),
        in_specs=whole(1) + [pl.BlockSpec(memory_space=pltpu.HBM)],
        out_specs=tuple(whole(2)),
        scratch_shapes=[
            pltpu.VMEM((TEAM, KEYS, ROWS), jnp.bfloat16),
            pltpu.SemaphoreType.DMA((TEAM,)),
        ],
        compiler_params=pltpu.CompilerParams(vmem_limit_bytes=16 * 1024 * 1024),
        name="query",
    )(lat, pltpu.with_memory_space_constraint(ds, pltpu.HBM))
    both = near + swap(far, "c").astype(jnp.float32)
    for_pair = both[ROWS:].astype(jnp.bfloat16)
    parts, for_pair = lax.optimization_barrier((parts, for_pair))
    from_pair = swap(for_pair, "y0")
    query_sum = both[:ROWS] + from_pair.astype(jnp.float32)
    query_grad = query_sum[:, :576].astype(jnp.bfloat16).reshape(queries.shape)

    tile_sum = call(sum_kernel, shape((128, WIDE), jnp.bfloat16), 0, 1, "sum")(parts)
    parts = exchange(tile_sum.reshape(16, 8, WIDE), ("zh", "yh"))
    latent_grad = jnp.sum(parts.astype(jnp.float32), axis=0)[:, :576]
    return (query_grad, latent_grad)


def solution(mesh):
    fine = Mesh(mesh.devices.reshape(SIZES), FINE)
    seq, head = FINE[:3], FINE[3:]
    placed = (
        P(seq, head, None),
        P(seq, None),
        P(seq, head, None),
        P(seq, head, None),
        P(seq),
    )
    return jax.shard_map(
        per_device,
        mesh=fine,
        in_specs=placed,
        out_specs=(P(seq, head, None), P(FINE, None)),
        check_vma=False,
    )
```

```python
import jax
import jax.numpy as jnp
from jax import lax
from jax.experimental import pallas as pl
from jax.experimental.pallas import tpu as pltpu
from jax.sharding import Mesh, PartitionSpec as P

score_scale = 192 ** (-0.5)
masked_score = -1e30
least_top = -1e29

ROWS = 256
WIDE = 640
VALUES = 512
PACK = 1152
KEYS = 1024
TILE = 256
PIECE = 64
FOLD = 288
TEAM = 4
TILES = KEYS // TILE

FINE = ("zh", "x", "c", "zl", "yh", "y0")
SIZES = (4, 4, 2, 2, 4, 2)


def prep_kernel(start_ref, q_ref, do_ref, lo_ref, out_ref):
    grad = do_ref[...]
    delta = jnp.sum(
        grad.astype(jnp.float32) * lo_ref[...].astype(jnp.float32), axis=1, keepdims=True
    )
    first = delta.astype(jnp.bfloat16).astype(jnp.float32)
    second = (delta - first).astype(jnp.bfloat16).astype(jnp.float32)
    third = delta - first - second
    pos = start_ref[0] + lax.broadcasted_iota(jnp.int32, (ROWS, 64), 0) // 8
    lane = lax.broadcasted_iota(jnp.int32, (ROWS, 64), 1)
    extra = jnp.where(lane == 0, first, 0.0)
    extra = jnp.where(lane == 1, second, extra)
    extra = jnp.where(lane == 2, third, extra)
    extra = jnp.where(lane == 3, (pos // 64).astype(jnp.float32), extra)
    extra = jnp.where(lane == 4, (pos % 64).astype(jnp.float32), extra)
    out_ref[:, :VALUES] = grad
    out_ref[:, VALUES:VALUES + 512] = q_ref[:, :512]
    out_ref[:, VALUES + 512:] = jnp.concatenate(
        [q_ref[:, 512:576], extra.astype(jnp.bfloat16)], axis=1
    )


def dot_nt(a, b):
    return lax.dot_general(a, b, (((1,), (1,)), ((), ())), preferred_element_type=jnp.float32)


def row_facts(block_ref):
    kind = lax.broadcasted_iota(jnp.int32, (8, 128), 0)
    lane = lax.broadcasted_iota(jnp.int32, (8, 128), 1) - 64
    pick = jnp.where((kind == 0) & (lane >= 0) & (lane <= 2), 1.0, 0.0)
    pick = jnp.where((kind == 1) & (lane == 3), 64.0, pick)
    pick = jnp.where((kind == 1) & (lane == 4), 1.0, pick)
    facts = dot_nt(pick.astype(jnp.bfloat16), block_ref[:, 1024:])
    return facts[0:1], facts[1:2]


def spread_kernel(place_ref, lat_ref, out_ref):
    odd = place_ref[0] % 2 == 1
    rows = lat_ref[...].T.reshape(8, 2, 8, 576)
    mine = jnp.where(odd, rows[:, 1], rows[:, 0]).reshape(PIECE, 576)
    folded = jnp.concatenate(
        [mine[:, 128 * j:128 * j + 128] for j in range(4)]
        + [jnp.concatenate([mine[:32, 512:], mine[32:, 512:]], axis=1)],
        axis=0,
    )
    for peer in range(4):
        out_ref[peer] = folded


def unfold(piece_ref):
    parts = [piece_ref[64 * j:64 * j + 64] for j in range(4)]
    tail = piece_ref[256:288]
    tail = jnp.concatenate([tail[:, :64], tail[:, 64:]], axis=0)
    return jnp.concatenate(parts + [tail, jnp.zeros((PIECE, 64), jnp.bfloat16)], axis=1)


def tile_rows(tile):
    return pl.ds(pl.multiple_of(tile * TILE, TILE), TILE)


def block_cols(k):
    return slice(k * ROWS, (k + 1) * ROWS)


def score_kernel(place_ref, piece_ref, x0, x1, x2, x3, p_ref, stat_ref, lat_ref, top_ref):
    blocks = (x0, x1, x2, x3)
    core, odd = place_ref[0] // 2, place_ref[0] % 2
    poses = [row_facts(b)[1] for b in blocks]

    tops, sums = [], []
    for tile in range(TILES):
        rows = slice(tile * TILE, tile * TILE + TILE)
        n = lax.broadcasted_iota(jnp.int32, (TILE, 1), 0)
        key_pos = (
            (n // 64) * 1024 + tile * 256 + core * 128 + ((n // 8) % 8) * 16 + odd * 8 + n % 8
        ).astype(jnp.float32)
        keys = jnp.concatenate([unfold(piece_ref.at[4 * tile + zh]) for zh in range(4)], axis=0)
        lat_ref[rows, :] = keys
        for k, block in enumerate(blocks):
            s = dot_nt(keys, block[:, VALUES:]) * score_scale
            s = jnp.where(key_pos <= poses[k], s, masked_score)
            top = jnp.maximum(jnp.max(s, axis=0, keepdims=True), least_top)
            p = jnp.exp(s - top)
            p_ref[rows, block_cols(k)] = p
            tops.append(top)
            sums.append(jnp.sum(p, axis=0, keepdims=True))
    all_tops, all_sums = [], []
    for k in range(TEAM):
        top = tops[k]
        for tile in range(1, TILES):
            top = jnp.maximum(top, tops[TEAM * tile + k])
        all_tops.append(top)
        all_sums.append(
            sum(
                sums[TEAM * tile + k] * jnp.exp(tops[TEAM * tile + k] - top)
                for tile in range(TILES)
            )
        )
    top_ref[...] = jnp.concatenate(tops, axis=0)
    stat_ref[...] = jnp.concatenate(all_tops + all_sums, axis=0)


def value_kernel(lat_ref, x0, x1, x2, x3, p_ref, t_ref):
    blocks = (x0, x1, x2, x3)
    deltas = [row_facts(b)[0] for b in blocks]

    def values(tile, _):
        rows = tile_rows(tile)
        held = lat_ref[rows, :VALUES]
        for k, block in enumerate(blocks):
            pg = dot_nt(held, block[:, :VALUES])
            t_ref[rows, block_cols(k)] = p_ref[rows, block_cols(k)] * (pg - deltas[k])
        return 0

    lax.fori_loop(0, KEYS // TILE, values, 0, unroll=True)


def row_factors(place_ref, own_ref, here_ref, there_ref):
    core = place_ref[0] // 2
    factors = []
    for k in range(TEAM):
        tops, sums = [], []
        for y, team_ref in enumerate((here_ref, there_ref)):
            for c in range(2):
                spot = (2 * c + y) ^ k
                tops.append(team_ref[core ^ c, spot:spot + 1, :])
                sums.append(team_ref[core ^ c, TEAM + spot:TEAM + spot + 1, :])
        top = jnp.maximum(jnp.maximum(tops[0], tops[1]), jnp.maximum(tops[2], tops[3]))
        total = sum(z * jnp.exp(m - top) for m, z in zip(tops, sums))
        inverse = 1.0 / total
        factors.append(
            [
                jnp.exp(own_ref[TEAM * t + k:TEAM * t + k + 1, :] - top) * inverse
                for t in range(TILES)
            ]
        )
    return factors


def key_kernel(
    place_ref, own_ref, here_ref, there_ref, x0, x1, x2, x3, p_ref, t_ref, key_ref, ds_ref,
    held_ref, held_ds, sems,
):
    blocks = (x0, x1, x2, x3)
    factors = row_factors(place_ref, own_ref, here_ref, there_ref)

    def leave(tile):
        part, rows = pl.ds(tile * 2, 2), tile_rows(tile)
        return (
            pltpu.make_async_copy(held_ref.at[part], key_ref.at[part], sems.at[0, tile]),
            pltpu.make_async_copy(held_ds.at[rows], ds_ref.at[rows], sems.at[1, tile]),
        )

    for tile in range(TILES):
        rows = slice(tile * TILE, tile * TILE + TILE)
        low = high = None
        for k, block in enumerate(blocks):
            cols = block_cols(k)
            w = (p_ref[rows, cols] * factors[k][tile]).astype(jnp.bfloat16)
            ds = (t_ref[rows, cols] * (factors[k][tile] * score_scale)).astype(jnp.bfloat16)
            held_ds[rows, cols] = ds
            part = jnp.dot(
                ds, block[:, VALUES:VALUES + 512], preferred_element_type=jnp.float32
            ) + jnp.dot(w, block[:, :VALUES], preferred_element_type=jnp.float32)
            tail = jnp.dot(ds, block[:, 1024:], preferred_element_type=jnp.float32)
            low = part if low is None else low + part
            high = tail if high is None else high + tail
        both = jnp.concatenate([low, high], axis=1)
        for zl in range(2):
            part = jnp.concatenate(
                [both[n:n + 32] for n in range(32 * zl, TILE, 64)], axis=0
            ).astype(held_ref.dtype)
            for j in range(4):
                held_ref[2 * tile + zl, 128 * j:128 * j + 128] = part[:, 128 * j:128 * j + 128]
            held_ref[2 * tile + zl, 512:] = jnp.concatenate(
                [part[:64, 512:576], part[64:, 512:576]], axis=1
            )
        for copy in leave(tile):
            copy.start()
    for tile in range(KEYS // TILE):
        for copy in leave(tile):
            copy.wait()


def query_kernel(lat_ref, ds_ref, near_ref, far_ref, held_ref, sems):
    def bring(k):
        return pltpu.make_async_copy(ds_ref.at[:, block_cols(k)], held_ref.at[k], sems.at[k])

    for k in range(TEAM):
        bring(k).start()
    for k in (2, 3, 0, 1):
        bring(k).wait()
        out = lax.dot_general(
            held_ref[k], lat_ref[...],
            (((0,), (0,)), ((), ())), preferred_element_type=jnp.float32,
        )
        ref = near_ref if k < 2 else far_ref
        ref[(k % 2) * ROWS:(k % 2 + 1) * ROWS, :] = out.astype(ref.dtype)


def sum_kernel(part_ref, out_ref):
    def total(rows):
        return sum(part_ref[peer, rows].astype(jnp.float32) for peer in range(8))

    for j in range(4):
        chunk = total(slice(128 * j, 128 * j + 128))
        out_ref[:, 128 * j:128 * j + 128] = chunk.astype(out_ref.dtype)
    tail = total(slice(512, 576))
    tail = jnp.concatenate([tail[:, :64], tail[:, 64:]], axis=0)
    tail = jnp.concatenate([tail, jnp.zeros_like(tail)], axis=1)
    out_ref[:, 512:] = tail.astype(out_ref.dtype)


def copy_kernel(rows_ref, out_ref, sems):
    copies = [
        pltpu.make_async_copy(rows_ref, out_ref.at[peer], sems.at[peer]) for peer in range(4)
    ]
    for copy in copies:
        copy.start()
    for copy in copies:
        copy.wait()


def whole(n):
    return [pl.BlockSpec(memory_space=pltpu.VMEM)] * n


SMEM = pl.BlockSpec(memory_space=pltpu.SMEM)


def swap(block, axis):
    return lax.ppermute(block, axis, [(0, 1), (1, 0)])


def exchange(pieces, axes):
    return lax.all_to_all(pieces, axes, 0, 0, tiled=True)


def call(kernel, out_shape, smem, vmem, name, limit=16):
    single = not isinstance(out_shape, tuple)
    return pl.pallas_call(
        kernel,
        out_shape=out_shape,
        in_specs=[SMEM] * smem + whole(vmem),
        out_specs=whole(1)[0] if single else tuple(whole(len(out_shape))),
        compiler_params=pltpu.CompilerParams(vmem_limit_bytes=limit * 1024 * 1024),
        name=name,
    )


def per_device(queries, latents, out_grad, layer_out, query_start):
    place = (lax.axis_index("c") * 2 + lax.axis_index("y0")).astype(jnp.int32).reshape(1)
    shape = jax.ShapeDtypeStruct

    pieces = call(spread_kernel, shape((4, FOLD, 128), jnp.bfloat16), 1, 1, "spread")(
        place, latents.T
    )
    pieces = exchange(pieces, ("zh",))
    pieces = pl.pallas_call(
        copy_kernel,
        out_shape=pltpu.HBM((4, 4, FOLD, 128), jnp.bfloat16),
        in_specs=whole(1),
        out_specs=pl.BlockSpec(memory_space=pltpu.HBM),
        scratch_shapes=[pltpu.SemaphoreType.DMA((4,))],
        compiler_params=pltpu.CompilerParams(vmem_limit_bytes=16 * 1024 * 1024),
        name="copies",
    )(pieces)
    pieces = exchange(pieces, ("x",))
    pieces = pieces.reshape(16, FOLD, 128)

    x0 = call(prep_kernel, shape((ROWS, PACK), jnp.bfloat16), 1, 3, "prep")(
        query_start,
        queries.reshape(ROWS, 576),
        out_grad.reshape(ROWS, VALUES),
        layer_out.reshape(ROWS, VALUES),
    )
    x1 = swap(x0, "y0")
    x2 = swap(x0, "c")
    x3 = swap(x1, "c")
    x = (x0, x1, x2, x3)

    square = shape((KEYS, TEAM * ROWS), jnp.float32)
    p, stats, lat, tops = call(
        score_kernel,
        (
            square,
            shape((2 * TEAM, ROWS), jnp.float32),
            shape((KEYS, WIDE), jnp.bfloat16),
            shape((TILES * TEAM, ROWS), jnp.float32),
        ),
        1, 5, "scores",
    )(place, pieces, *x)
    here = lax.all_gather(stats, "c", axis=0, tiled=False)
    there = swap(here, "y0")
    t = call(value_kernel, square, 0, 6, "values")(lat, *x, p)

    key_part, ds = pl.pallas_call(
        key_kernel,
        out_shape=(
            pltpu.HBM((8, 576, 128), jnp.bfloat16),
            pltpu.HBM((KEYS, TEAM * ROWS), jnp.bfloat16),
        ),
        in_specs=[SMEM] + whole(9),
        out_specs=(pl.BlockSpec(memory_space=pltpu.HBM),) * 2,
        scratch_shapes=[
            pltpu.VMEM((8, 576, 128), jnp.bfloat16),
            pltpu.VMEM((KEYS, TEAM * ROWS), jnp.bfloat16),
            pltpu.SemaphoreType.DMA((2, KEYS // TILE)),
        ],
        compiler_params=pltpu.CompilerParams(vmem_limit_bytes=16 * 1024 * 1024),
        name="keys",
    )(place, tops, here, there, *x, p, t)
    parts = exchange(key_part, ("x", "zl"))

    near, far = pl.pallas_call(
        query_kernel,
        out_shape=(
            shape((2 * ROWS, WIDE), jnp.float32),
            shape((2 * ROWS, WIDE), jnp.bfloat16),
        ),
        in_specs=whole(1) + [pl.BlockSpec(memory_space=pltpu.HBM)],
        out_specs=tuple(whole(2)),
        scratch_shapes=[
            pltpu.VMEM((TEAM, KEYS, ROWS), jnp.bfloat16),
            pltpu.SemaphoreType.DMA((TEAM,)),
        ],
        compiler_params=pltpu.CompilerParams(vmem_limit_bytes=16 * 1024 * 1024),
        name="query",
    )(lat, pltpu.with_memory_space_constraint(ds, pltpu.HBM))
    both = near + swap(far, "c").astype(jnp.float32)
    for_pair = both[ROWS:].astype(jnp.bfloat16)
    parts, for_pair = lax.optimization_barrier((parts, for_pair))
    from_pair = swap(for_pair, "y0")
    query_sum = both[:ROWS] + from_pair.astype(jnp.float32)
    query_grad = query_sum[:, :576].astype(jnp.bfloat16).reshape(queries.shape)

    tile_sum = call(sum_kernel, shape((128, WIDE), jnp.bfloat16), 0, 1, "sum")(parts)
    parts = exchange(tile_sum.reshape(16, 8, WIDE), ("zh", "yh"))
    latent_grad = jnp.sum(parts.astype(jnp.float32), axis=0)[:, :576]
    return (query_grad, latent_grad)


def solution(mesh):
    fine = Mesh(mesh.devices.reshape(SIZES), FINE)
    seq, head = FINE[:3], FINE[3:]
    placed = (
        P(seq, head, None),
        P(seq, None),
        P(seq, head, None),
        P(seq, head, None),
        P(seq),
    )
    return jax.shard_map(
        per_device,
        mesh=fine,
        in_specs=placed,
        out_specs=(P(seq, head, None), P(FINE, None)),
        check_vma=False,
    )
```

```python
import jax
import jax.numpy as jnp
from jax import lax
from jax.experimental import pallas as pl
from jax.experimental.pallas import tpu as pltpu
from jax.sharding import Mesh, PartitionSpec as P

score_scale = 192 ** (-0.5)
masked_score = -1e30
least_top = -1e29

ROWS = 256
WIDE = 640
VALUES = 512
PACK = 1152
KEYS = 1024
TILE = 256
PIECE = 64
FOLD = 288
TEAM = 4
TILES = KEYS // TILE

FINE = ("zh", "x", "c", "zl", "yh", "y0")
SIZES = (4, 4, 2, 2, 4, 2)


def prep_kernel(start_ref, far_q, far_do, far_lo, out_ref, q_ref, do_ref, lo_ref, sems):
    copies = [
        pltpu.make_async_copy(far, near, sems.at[i])
        for i, (far, near) in enumerate(((far_q, q_ref), (far_do, do_ref), (far_lo, lo_ref)))
    ]
    for copy in copies:
        copy.start()
    for copy in copies:
        copy.wait()
    grad = do_ref[...]
    delta = jnp.sum(
        grad.astype(jnp.float32) * lo_ref[...].astype(jnp.float32), axis=1, keepdims=True
    )
    first = delta.astype(jnp.bfloat16).astype(jnp.float32)
    second = (delta - first).astype(jnp.bfloat16).astype(jnp.float32)
    third = delta - first - second
    pos = start_ref[0] + lax.broadcasted_iota(jnp.int32, (ROWS, 64), 0) // 8
    lane = lax.broadcasted_iota(jnp.int32, (ROWS, 64), 1)
    extra = jnp.where(lane == 0, first, 0.0)
    extra = jnp.where(lane == 1, second, extra)
    extra = jnp.where(lane == 2, third, extra)
    extra = jnp.where(lane == 3, (pos // 64).astype(jnp.float32), extra)
    extra = jnp.where(lane == 4, (pos % 64).astype(jnp.float32), extra)
    out_ref[:, :VALUES] = grad
    out_ref[:, VALUES:VALUES + 512] = q_ref[:, :512]
    out_ref[:, VALUES + 512:] = jnp.concatenate(
        [q_ref[:, 512:576], extra.astype(jnp.bfloat16)], axis=1
    )


def dot_nt(a, b):
    return lax.dot_general(a, b, (((1,), (1,)), ((), ())), preferred_element_type=jnp.float32)


def row_facts(block_ref):
    kind = lax.broadcasted_iota(jnp.int32, (8, 128), 0)
    lane = lax.broadcasted_iota(jnp.int32, (8, 128), 1) - 64
    pick = jnp.where((kind == 0) & (lane >= 0) & (lane <= 2), 1.0, 0.0)
    pick = jnp.where((kind == 1) & (lane == 3), 64.0, pick)
    pick = jnp.where((kind == 1) & (lane == 4), 1.0, pick)
    facts = dot_nt(pick.astype(jnp.bfloat16), block_ref[:, 1024:])
    return facts[0:1], facts[1:2]


def spread_kernel(place_ref, lat_ref, out_ref):
    odd = place_ref[0] % 2 == 1
    rows = lat_ref[...].T.reshape(8, 2, 8, 576)
    mine = jnp.where(odd, rows[:, 1], rows[:, 0]).reshape(PIECE, 576)
    folded = jnp.concatenate(
        [mine[:, 128 * j:128 * j + 128] for j in range(4)]
        + [jnp.concatenate([mine[:32, 512:], mine[32:, 512:]], axis=1)],
        axis=0,
    )
    for peer in range(4):
        out_ref[peer] = folded


def unfold(piece_ref):
    parts = [piece_ref[64 * j:64 * j + 64] for j in range(4)]
    tail = piece_ref[256:288]
    tail = jnp.concatenate([tail[:, :64], tail[:, 64:]], axis=0)
    return jnp.concatenate(parts + [tail, jnp.zeros((PIECE, 64), jnp.bfloat16)], axis=1)


def tile_rows(tile):
    return pl.ds(pl.multiple_of(tile * TILE, TILE), TILE)


def block_cols(k):
    return slice(k * ROWS, (k + 1) * ROWS)


def score_kernel(place_ref, piece_ref, x0, x1, x2, x3, p_ref, stat_ref, lat_ref, top_ref):
    blocks = (x0, x1, x2, x3)
    core, odd = place_ref[0] // 2, place_ref[0] % 2
    poses = [row_facts(b)[1] for b in blocks]

    tops, sums = [], []
    for tile in range(TILES):
        rows = slice(tile * TILE, tile * TILE + TILE)
        n = lax.broadcasted_iota(jnp.int32, (TILE, 1), 0)
        key_pos = (
            (n // 64) * 1024 + tile * 256 + core * 128 + ((n // 8) % 8) * 16 + odd * 8 + n % 8
        ).astype(jnp.float32)
        keys = jnp.concatenate([unfold(piece_ref.at[4 * tile + zh]) for zh in range(4)], axis=0)
        lat_ref[rows, :] = keys
        for k, block in enumerate(blocks):
            s = dot_nt(keys, block[:, VALUES:]) * score_scale
            s = jnp.where(key_pos <= poses[k], s, masked_score)
            top = jnp.maximum(jnp.max(s, axis=0, keepdims=True), least_top)
            p = jnp.exp(s - top)
            p_ref[rows, block_cols(k)] = p
            tops.append(top)
            sums.append(jnp.sum(p, axis=0, keepdims=True))
    all_tops, all_sums = [], []
    for k in range(TEAM):
        top = tops[k]
        for tile in range(1, TILES):
            top = jnp.maximum(top, tops[TEAM * tile + k])
        all_tops.append(top)
        all_sums.append(
            sum(
                sums[TEAM * tile + k] * jnp.exp(tops[TEAM * tile + k] - top)
                for tile in range(TILES)
            )
        )
    top_ref[...] = jnp.concatenate(tops, axis=0)
    stat_ref[...] = jnp.concatenate(all_tops + all_sums, axis=0)


def value_kernel(lat_ref, x0, x1, x2, x3, p_ref, t_ref):
    blocks = (x0, x1, x2, x3)
    deltas = [row_facts(b)[0] for b in blocks]

    def values(tile, _):
        rows = tile_rows(tile)
        held = lat_ref[rows, :VALUES]
        for k, block in enumerate(blocks):
            pg = dot_nt(held, block[:, :VALUES])
            t_ref[rows, block_cols(k)] = p_ref[rows, block_cols(k)] * (pg - deltas[k])
        return 0

    lax.fori_loop(0, KEYS // TILE, values, 0, unroll=True)


def row_factors(place_ref, own_ref, here_ref, there_ref):
    core = place_ref[0] // 2
    factors = []
    for k in range(TEAM):
        tops, sums = [], []
        for y, team_ref in enumerate((here_ref, there_ref)):
            for c in range(2):
                spot = (2 * c + y) ^ k
                tops.append(team_ref[core ^ c, spot:spot + 1, :])
                sums.append(team_ref[core ^ c, TEAM + spot:TEAM + spot + 1, :])
        top = jnp.maximum(jnp.maximum(tops[0], tops[1]), jnp.maximum(tops[2], tops[3]))
        total = sum(z * jnp.exp(m - top) for m, z in zip(tops, sums))
        inverse = 1.0 / total
        factors.append(
            [
                jnp.exp(own_ref[TEAM * t + k:TEAM * t + k + 1, :] - top) * inverse
                for t in range(TILES)
            ]
        )
    return factors


def key_kernel(
    place_ref, own_ref, here_ref, there_ref, x0, x1, x2, x3, p_ref, t_ref, key_ref, ds_ref,
    held_ref, held_ds, sems,
):
    blocks = (x0, x1, x2, x3)
    factors = row_factors(place_ref, own_ref, here_ref, there_ref)

    def leave(tile):
        part, rows = pl.ds(tile * 2, 2), tile_rows(tile)
        return (
            pltpu.make_async_copy(held_ref.at[part], key_ref.at[part], sems.at[0, tile]),
            pltpu.make_async_copy(held_ds.at[rows], ds_ref.at[rows], sems.at[1, tile]),
        )

    for tile in range(TILES):
        rows = slice(tile * TILE, tile * TILE + TILE)
        low = high = None
        for k, block in enumerate(blocks):
            cols = block_cols(k)
            w = (p_ref[rows, cols] * factors[k][tile]).astype(jnp.bfloat16)
            ds = (t_ref[rows, cols] * (factors[k][tile] * score_scale)).astype(jnp.bfloat16)
            held_ds[rows, cols] = ds
            part = jnp.dot(
                ds, block[:, VALUES:VALUES + 512], preferred_element_type=jnp.float32
            ) + jnp.dot(w, block[:, :VALUES], preferred_element_type=jnp.float32)
            tail = jnp.dot(ds, block[:, 1024:], preferred_element_type=jnp.float32)
            low = part if low is None else low + part
            high = tail if high is None else high + tail
        both = jnp.concatenate([low, high], axis=1)
        for zl in range(2):
            part = jnp.concatenate(
                [both[n:n + 32] for n in range(32 * zl, TILE, 64)], axis=0
            ).astype(held_ref.dtype)
            for j in range(4):
                held_ref[2 * tile + zl, 128 * j:128 * j + 128] = part[:, 128 * j:128 * j + 128]
            held_ref[2 * tile + zl, 512:] = jnp.concatenate(
                [part[:64, 512:576], part[64:, 512:576]], axis=1
            )
        for copy in leave(tile):
            copy.start()
    for tile in range(KEYS // TILE):
        for copy in leave(tile):
            copy.wait()


def query_kernel(lat_ref, ds_ref, near_ref, far_ref, held_ref, sems):
    def bring(k):
        return pltpu.make_async_copy(ds_ref.at[:, block_cols(k)], held_ref.at[k], sems.at[k])

    for k in range(TEAM):
        bring(k).start()
    for k in (2, 3, 0, 1):
        bring(k).wait()
        out = lax.dot_general(
            held_ref[k], lat_ref[...],
            (((0,), (0,)), ((), ())), preferred_element_type=jnp.float32,
        )
        ref = near_ref if k < 2 else far_ref
        ref[(k % 2) * ROWS:(k % 2 + 1) * ROWS, :] = out.astype(ref.dtype)


def sum_kernel(part_ref, out_ref):
    def total(rows):
        return sum(part_ref[peer, rows].astype(jnp.float32) for peer in range(8))

    for j in range(4):
        chunk = total(slice(128 * j, 128 * j + 128))
        out_ref[:, 128 * j:128 * j + 128] = chunk.astype(out_ref.dtype)
    tail = total(slice(512, 576))
    tail = jnp.concatenate([tail[:, :64], tail[:, 64:]], axis=0)
    tail = jnp.concatenate([tail, jnp.zeros_like(tail)], axis=1)
    out_ref[:, 512:] = tail.astype(out_ref.dtype)


def copy_kernel(rows_ref, out_ref, sems):
    copies = [
        pltpu.make_async_copy(rows_ref, out_ref.at[peer], sems.at[peer]) for peer in range(4)
    ]
    for copy in copies:
        copy.start()
    for copy in copies:
        copy.wait()


def whole(n):
    return [pl.BlockSpec(memory_space=pltpu.VMEM)] * n


SMEM = pl.BlockSpec(memory_space=pltpu.SMEM)


def swap(block, axis):
    return lax.ppermute(block, axis, [(0, 1), (1, 0)])


def exchange(pieces, axes):
    return lax.all_to_all(pieces, axes, 0, 0, tiled=True)


def call(kernel, out_shape, smem, vmem, name, limit=16):
    single = not isinstance(out_shape, tuple)
    return pl.pallas_call(
        kernel,
        out_shape=out_shape,
        in_specs=[SMEM] * smem + whole(vmem),
        out_specs=whole(1)[0] if single else tuple(whole(len(out_shape))),
        compiler_params=pltpu.CompilerParams(vmem_limit_bytes=limit * 1024 * 1024),
        name=name,
    )


def per_device(queries, latents, out_grad, layer_out, query_start):
    place = (lax.axis_index("c") * 2 + lax.axis_index("y0")).astype(jnp.int32).reshape(1)
    shape = jax.ShapeDtypeStruct

    pieces = call(spread_kernel, shape((4, FOLD, 128), jnp.bfloat16), 1, 1, "spread")(
        place, latents.T
    )
    pieces = exchange(pieces, ("zh",))
    pieces = pl.pallas_call(
        copy_kernel,
        out_shape=pltpu.HBM((4, 4, FOLD, 128), jnp.bfloat16),
        in_specs=whole(1),
        out_specs=pl.BlockSpec(memory_space=pltpu.HBM),
        scratch_shapes=[pltpu.SemaphoreType.DMA((4,))],
        compiler_params=pltpu.CompilerParams(vmem_limit_bytes=16 * 1024 * 1024),
        name="copies",
    )(pieces)
    pieces = exchange(pieces, ("x",))
    pieces = pieces.reshape(16, FOLD, 128)

    own = [
        pltpu.with_memory_space_constraint(array, pltpu.HBM)
        for array in (
            queries.reshape(ROWS, 576),
            out_grad.reshape(ROWS, VALUES),
            layer_out.reshape(ROWS, VALUES),
        )
    ]
    x0 = pl.pallas_call(
        prep_kernel,
        out_shape=shape((ROWS, PACK), jnp.bfloat16),
        in_specs=[SMEM] + [pl.BlockSpec(memory_space=pltpu.HBM)] * 3,
        out_specs=whole(1)[0],
        scratch_shapes=[pltpu.VMEM(array.shape, array.dtype) for array in own]
        + [pltpu.SemaphoreType.DMA((3,))],
        compiler_params=pltpu.CompilerParams(vmem_limit_bytes=16 * 1024 * 1024),
        name="prep",
    )(query_start, *own)
    x1 = swap(x0, "y0")
    x2 = swap(x0, "c")
    x3 = swap(x1, "c")
    x = (x0, x1, x2, x3)

    square = shape((KEYS, TEAM * ROWS), jnp.float32)
    p, stats, lat, tops = call(
        score_kernel,
        (
            square,
            shape((2 * TEAM, ROWS), jnp.float32),
            shape((KEYS, WIDE), jnp.bfloat16),
            shape((TILES * TEAM, ROWS), jnp.float32),
        ),
        1, 5, "scores",
    )(place, pieces, *x)
    here = lax.all_gather(stats, "c", axis=0, tiled=False)
    there = swap(here, "y0")
    t = call(value_kernel, square, 0, 6, "values")(lat, *x, p)

    key_part, ds = pl.pallas_call(
        key_kernel,
        out_shape=(
            pltpu.HBM((8, 576, 128), jnp.bfloat16),
            pltpu.HBM((KEYS, TEAM * ROWS), jnp.bfloat16),
        ),
        in_specs=[SMEM] + whole(9),
        out_specs=(pl.BlockSpec(memory_space=pltpu.HBM),) * 2,
        scratch_shapes=[
            pltpu.VMEM((8, 576, 128), jnp.bfloat16),
            pltpu.VMEM((KEYS, TEAM * ROWS), jnp.bfloat16),
            pltpu.SemaphoreType.DMA((2, KEYS // TILE)),
        ],
        compiler_params=pltpu.CompilerParams(vmem_limit_bytes=16 * 1024 * 1024),
        name="keys",
    )(place, tops, here, there, *x, p, t)
    parts = exchange(key_part, ("x", "zl"))

    near, far = pl.pallas_call(
        query_kernel,
        out_shape=(
            shape((2 * ROWS, WIDE), jnp.float32),
            shape((2 * ROWS, WIDE), jnp.bfloat16),
        ),
        in_specs=whole(1) + [pl.BlockSpec(memory_space=pltpu.HBM)],
        out_specs=tuple(whole(2)),
        scratch_shapes=[
            pltpu.VMEM((TEAM, KEYS, ROWS), jnp.bfloat16),
            pltpu.SemaphoreType.DMA((TEAM,)),
        ],
        compiler_params=pltpu.CompilerParams(vmem_limit_bytes=16 * 1024 * 1024),
        name="query",
    )(lat, pltpu.with_memory_space_constraint(ds, pltpu.HBM))
    both = near + swap(far, "c").astype(jnp.float32)
    for_pair = both[ROWS:].astype(jnp.bfloat16)
    parts, for_pair = lax.optimization_barrier((parts, for_pair))
    from_pair = swap(for_pair, "y0")
    query_sum = both[:ROWS] + from_pair.astype(jnp.float32)
    query_grad = query_sum[:, :576].astype(jnp.bfloat16).reshape(queries.shape)

    tile_sum = call(sum_kernel, shape((128, WIDE), jnp.bfloat16), 0, 1, "sum")(parts)
    parts = exchange(tile_sum.reshape(16, 8, WIDE), ("zh", "yh"))
    latent_grad = jnp.sum(parts.astype(jnp.float32), axis=0)[:, :576]
    return (query_grad, latent_grad)


def solution(mesh):
    fine = Mesh(mesh.devices.reshape(SIZES), FINE)
    seq, head = FINE[:3], FINE[3:]
    placed = (
        P(seq, head, None),
        P(seq, None),
        P(seq, head, None),
        P(seq, head, None),
        P(seq),
    )
    return jax.shard_map(
        per_device,
        mesh=fine,
        in_specs=placed,
        out_specs=(P(seq, head, None), P(FINE, None)),
        check_vma=False,
    )
```
